512 devices in a mesh: wide: 32 (over z_lo, x), narrow: 16 (over y, z_hi, core).
Axes of the slice: x: 4, y: 4, z: 16 (z_hi: 2, z_lo: 8; z = z_hi * 8 + z_lo), core: 2. Of those that a mesh axis runs over, the one named last changes fastest.
Arguments:
- a_blocks: bfloat16 [8192, 7, 4096], P(('wide', 'narrow')), may hold values from -0.25 to 0.25
- p_blocks: bfloat16 [8192, 4096], P(('wide', 'narrow')), may hold values from -0.75 to 0.75
- columns: int32 [8192, 7], P(('wide', 'narrow')), may hold values from 0 to 8191, as said below
- aggregate: int32 [8192], P(('wide', 'narrow')), may hold values from 0 to 511, as said below
- target: int32 [8192, 7], P(('wide', 'narrow')), may hold values from 0 to 6
Outputs:
- coarse: float32 [512, 7, 4096], P(('wide', 'narrow'))
The draws below stay inside these ranges and needn't reach their ends.
Inputs may be any that keep to these rules, and one draw needn't show every extreme that they name: columns[i,0] = i; every entry lies within 16 of its row i, and entries i + 16 or i - 16 occur in every row. Fine block row i belongs to an aggregate of its own pair of planes: aggregate[i] // 2 = i // 32; every aggregate has a fine block row.
All inputs are finite; a program needn't handle non-finite values.
Results may differ from the reference program's by a relative error of at most 0.0029.
Values may be sent and summed in bfloat16 or wider, within the bound.
A program may use at most 64 MiB of HBM per device.

```python
import jax
import jax.numpy as jnp
from jax import lax

B = 64
K = 7
KC = 7
CR_DEV = 1
PLANE = 16
NF = 8192
NC = 512


def draw_columns(key, part):
    key = jax.random.fold_in(key, 7)
    fine_rows = jnp.arange(NF, dtype=jnp.int32)
    random_offsets = jax.random.randint(key, (NF, K - 3), -PLANE, PLANE + 1).astype(jnp.int32)
    fixed_offsets = jnp.broadcast_to(jnp.array([0, PLANE, -PLANE], dtype=jnp.int32), (NF, 3))
    offsets = jnp.concatenate([fixed_offsets, random_offsets], axis=1)
    raw_cols = fine_rows[:, None] + offsets
    outside = (raw_cols < 0) | (raw_cols >= NF)
    return jnp.where(outside, fine_rows[:, None] - offsets, raw_cols).astype(jnp.int32)


def draw_aggregate(key, part):
    key = jax.random.fold_in(key, 11)
    fine_rows = jnp.arange(NF, dtype=jnp.int32)
    pair_count = 2 * CR_DEV
    pair_index = fine_rows // (2 * PLANE)
    within_plane = fine_rows % PLANE
    plane_parity = fine_rows // PLANE % 2
    box_width = PLANE // pair_count
    box_index = within_plane // box_width
    jitter = jax.random.randint(key, (NF,), -1, 2).astype(jnp.int32)
    anchor = (within_plane % box_width == 0) & (plane_parity == 0)
    moved = jnp.clip(box_index + jitter, 0, pair_count - 1)
    chosen = jnp.where(anchor, box_index, moved)
    return (pair_index * pair_count + chosen).astype(jnp.int32)


def plant(result, key, least, top_value):
    place = [jax.random.randint(jax.random.fold_in(key, axis), (), 0, length) for axis, length in enumerate(result.shape)]
    longest = result.shape.index(max(result.shape))
    neighbour = place[:longest] + [(place[longest] + 1) % result.shape[longest]] + place[longest + 1:]
    return result.at[tuple(place)].set(least).at[tuple(neighbour)].set(top_value)


def level_of(stream_key, dims, shards, least, top_value):
    level = 1.0
    for dim, parts in shards:
        heights = jax.random.uniform(jax.random.fold_in(jax.random.fold_in(stream_key, 6), dim), (parts,), jnp.float32, least / len(shards), top_value / len(shards))
        level = level * jnp.repeat(jnp.exp(heights), dims[dim] // parts).reshape((-1,) + (1,) * (len(dims) - 1 - dim))
    return level


def bell_draw(key, extent, deviation, most, pieces=(), kind=jnp.bfloat16):
    loudness = level_of(key, extent, pieces, -0.22, 0.18) if pieces else 1.0
    values = jax.random.normal(key, extent, jnp.float32) * deviation * loudness
    return jnp.minimum(jnp.maximum(values, -most), most).astype(kind)


def setup_inputs(seed: int = 0) -> dict:
    splits = jax.random.split(jax.random.key(seed), 6)
    return {
        "a_blocks": bell_draw(splits[0], (NF, K, B * B), (B * K) ** -0.5, 0.25, ((0, 512),)),
        "p_blocks": bell_draw(splits[1], (NF, B * B), B ** -0.5, 0.75, ((0, 512),)),
        "columns": draw_columns(jax.random.fold_in(splits[5], 71), 0),
        "aggregate": draw_aggregate(jax.random.fold_in(splits[5], 71), 0),
        "target": plant(jax.random.randint(splits[4], (NF, K), 0, KC), jax.random.fold_in(splits[4], 1), 0, KC - 1).astype(jnp.int32),
    }


def reference(a_blocks, p_blocks, columns, aggregate, target):
    def one_row(packed):
        a_row, p_row, col_row = packed
        near = p_blocks[col_row].astype(jnp.float32).reshape(K, B, B)
        applied = jnp.einsum('kcd,kde->kce', a_row.astype(jnp.float32).reshape(K, B, B), near).astype(jnp.bfloat16)
        product = jnp.einsum('ca,kcb->kab', p_row.astype(jnp.float32).reshape(B, B), applied.astype(jnp.float32))
        return product.reshape(K, B * B)

    products = lax.map(one_row, (a_blocks, p_blocks, columns))
    slot_keys = (aggregate[:, None] * KC + target).reshape(-1).astype(jnp.int32)
    summed = jax.ops.segment_sum(products.reshape(NF * K, B * B), slot_keys, num_segments=NC * KC)
    return summed.reshape(NC, KC, B * B)
```

```python
import functools

import jax
import jax.numpy as jnp
from jax import lax
from jax.experimental import pallas as pl
from jax.experimental.pallas import tpu as pltpu
from jax.sharding import PartitionSpec as P

B = 64
K = 7
KC = 7
ROWS = 16
TILES = 32
LANES = 128
PAIRS = ((1, 2), (3, 4), (5, 6), (0, None))
GROUP = 4
X_CHIPS = 4
CHUNKS = 4
F32 = jnp.float32
BF16 = jnp.bfloat16
MESH = pl.DeviceIdType.MESH


def swap(x):
    return pltpu.roll(x, B, 1)


def kernel(
    n_wide,
    n_narrow,
    cols_hbm,
    agg_hbm,
    targ_hbm,
    p_hbm,
    a_hbm,
    out,
    cols,
    agg,
    targ,
    p_raw,
    a_raw,
    p_f32,
    a_f32,
    pair_f32,
    own_pairs,
    sib_pairs,
    passing,
    far_pairs,
    near_left,
    near_right,
    far_left,
    far_right,
    blocks,
    y_all,
    pm_f32,
    pm_t,
    acc,
    part_out,
    part_in,
    load_sem,
    send_sem,
    recv_sem,
):
    total = n_wide * n_narrow
    me = lax.axis_index("wide") * n_narrow + lax.axis_index("narrow")
    core = me % 2

    def place(index):
        return (index // n_narrow, index % n_narrow)

    def far_of(index):
        return (index - 1 + 2 * (index % 2) + total) % total

    def relay_of(index, flipped):
        wide, narrow = index // n_narrow, index % n_narrow
        z_lo, x = wide // X_CHIPS, wide % X_CHIPS
        flip = (z_lo + index % 2 + flipped) % 2
        z_hi = narrow // 2 % 2
        wide = (z_lo + 1 - 2 * (z_lo % 2)) * X_CHIPS + x
        return wide * n_narrow + narrow + flip * (2 - 4 * z_hi)

    partner = far_of(me)
    source = relay_of(me, 1)
    quick = (me // n_narrow // X_CHIPS + core) % 2 == 1
    sibling = place(me + 1 - 2 * core)
    relay = place(relay_of(me, 0))
    onward = place(far_of(source))

    barrier = pltpu.get_barrier_semaphore()
    for other in (sibling, place(source), place(relay_of(partner, 0))):
        pl.semaphore_signal(barrier, inc=1, device_id=other, device_id_type=MESH)
    operands = ((p_hbm, p_raw), (a_hbm, a_raw), (cols_hbm, cols), (agg_hbm, agg), (targ_hbm, targ))
    loads = [
        pltpu.make_async_copy(source, dest, load_sem.at[n])
        for n, (source, dest) in enumerate(operands)
    ]
    for load in loads:
        load.start()

    low = lax.broadcasted_iota(jnp.int32, (TILES, LANES), 1) < B
    low_block = lax.broadcasted_iota(jnp.int32, (B, LANES), 1) < B
    low_row = low[:8]

    loads[0].wait()
    for t in range(TILES):
        p_f32[pl.ds(t * ROWS, ROWS), :] = p_raw[:, pl.ds(t * LANES, LANES)].astype(F32)
    for j in range(ROWS // 2):
        one = p_f32[pl.ds(j, TILES, stride=ROWS), :]
        two = p_f32[pl.ds(j + 8, TILES, stride=ROWS), :]
        pair_f32[pl.ds(j * B, TILES, stride=2), :] = jnp.where(low, one, swap(two))
        pair_f32[pl.ds(j * B + 1, TILES, stride=2), :] = jnp.where(low, swap(one), two)
    for j in range(ROWS // 2):
        own_pairs[j] = pair_f32[pl.ds(j * B, B), :].astype(BF16)

    pl.semaphore_wait(barrier, 3)
    step = ROWS // 2 // CHUNKS
    chunks = [pl.ds(n * step, step) for n in range(CHUNKS)]
    to_relay = [
        pltpu.make_async_remote_copy(
            own_pairs.at[chunk],
            passing.at[chunk],
            send_sem.at[2 + n],
            recv_sem.at[2 + n],
            device_id=relay,
            device_id_type=MESH,
        )
        for n, chunk in enumerate(chunks)
    ]
    to_onward = [
        pltpu.make_async_remote_copy(
            passing.at[chunk],
            far_pairs.at[chunk],
            send_sem.at[2 + CHUNKS + n],
            recv_sem.at[2 + CHUNKS + n],
            device_id=onward,
            device_id_type=MESH,
        )
        for n, chunk in enumerate(chunks)
    ]
    to_sib = pltpu.make_async_remote_copy(
        own_pairs, sib_pairs, send_sem.at[1], recv_sem.at[1], device_id=sibling, device_id_type=MESH
    )
    for copy in to_relay:
        copy.start()
    to_sib.start()

    def pass_on():
        for n in range(CHUNKS):
            to_relay[n].wait_recv()
            to_onward[n].start()

    def unpack(source, left, right, start):
        def one(j, carry):
            both = source[j].astype(F32)
            turned = swap(both)
            left[start + j] = jnp.where(low_block, both, 0.0).astype(BF16)
            right[start + j] = jnp.where(low_block, 0.0, turned).astype(BF16)
            left[start + j + 8] = jnp.where(low_block, turned, 0.0).astype(BF16)
            right[start + j + 8] = jnp.where(low_block, 0.0, both).astype(BF16)
            return carry

        lax.fori_loop(0, ROWS // 2, one, 0)

    unpack(own_pairs, near_left, near_right, 0)
    pl.when(quick)(pass_on)
    for ref, end in (
        (near_left, 2 * ROWS),
        (near_right, 2 * ROWS),
        (far_left, ROWS),
        (far_right, ROWS),
    ):
        ref[end] = jnp.zeros((B, LANES), BF16)

    loads[1].wait()

    def widen(k, carry):
        for t in range(TILES):
            a_f32[pl.ds(k * TILES * ROWS + t * ROWS, ROWS), :] = a_raw[
                k, :, pl.ds(t * LANES, LANES)
            ].astype(F32)
        return carry

    lax.fori_loop(0, K, widen, 0)

    def arrange(i, carry):
        for n, (k, other) in enumerate(PAIRS):
            one = a_f32[pl.ds(k * TILES * ROWS + i, TILES, stride=ROWS), :]
            if other is None:
                even = jnp.where(low, one, 0.0)
                odd = jnp.where(low, swap(one), 0.0)
            else:
                two = a_f32[pl.ds(other * TILES * ROWS + i, TILES, stride=ROWS), :]
                even = jnp.where(low, one, swap(two))
                odd = jnp.where(low, swap(one), two)
            blocks[i * len(PAIRS) + n] = jnp.concatenate([even, odd], axis=0).astype(BF16)
        return carry

    lax.fori_loop(0, ROWS, arrange, 0)

    for load in loads[2:]:
        load.wait()
    first = me - core

    def transpose(pair, carry):
        halves = []
        for i in (2 * pair, 2 * pair + 1):
            x = p_f32[pl.ds(i, TILES, stride=ROWS), :]
            y = swap(x)
            keep = [jnp.where(agg[i] == first + c, 1.0, 0.0) for c in range(2)]
            halves.append(jnp.where(low, x * keep[0], y * keep[1]))
            halves.append(jnp.where(low, y * keep[0], x * keep[1]))
        pm_f32[...] = jnp.concatenate(halves, axis=0).T
        rows = [pm_f32[pl.ds(c * B + h, TILES, stride=2), :] for c in range(2) for h in range(2)]
        pm_t[pair] = jnp.concatenate(rows, axis=0).astype(BF16)
        return carry

    lax.fori_loop(0, ROWS // 2, transpose, 0)

    root = (me - 1) * ROWS

    def near_index(at):
        plane, at = at // ROWS, at % ROWS
        return jnp.where(plane == 1, at, jnp.where(plane == 2 - 2 * core, at + ROWS, 2 * ROWS))

    def far_index(at):
        plane, at = at // ROWS, at % ROWS
        return jnp.where(plane == 2 * core, at, ROWS)

    def multiply(pairs, left, right, index_of, initial):
        def group(g, carry):
            for r in range(GROUP):
                i = g * GROUP + r
                applied, slots = [], []
                for n, (k, other) in pairs:
                    above = left[index_of(cols[k, i] - root)]
                    slot = jnp.full((8, LANES), targ[k, i], jnp.int32)
                    if other is None:
                        below = jnp.zeros((B, LANES), BF16)
                    else:
                        below = right[index_of(cols[other, i] - root)]
                        slot = jnp.where(low_row, slot, targ[other, i])
                    applied.append(
                        jnp.dot(
                            blocks[i * len(PAIRS) + n],
                            jnp.concatenate([above, below], axis=0),
                            preferred_element_type=F32,
                        )
                    )
                    slots.append(slot)
                for s in range(KC):
                    summed = None
                    for value, slot in zip(applied, slots):
                        mask = jnp.concatenate([jnp.where(slot == s, 1.0, 0.0)] * 8, axis=0)
                        term = value * mask
                        summed = term if summed is None else summed + term
                    y_all[r, :, pl.ds(s * LANES, LANES)] = summed.astype(BF16)
            weights = jnp.concatenate(
                [pm_t[g * (GROUP // 2) + n] for n in range(GROUP // 2)], axis=1
            )
            partial = jnp.dot(
                weights,
                y_all[...].reshape(GROUP * B, KC * LANES),
                preferred_element_type=F32,
            )
            acc[...] += partial
            return carry

        if initial:
            acc[...] = jnp.zeros_like(acc)
        lax.fori_loop(0, ROWS // GROUP, group, 0)

    numbered = list(enumerate(PAIRS))
    to_sib.wait_recv()
    unpack(sib_pairs, near_left, near_right, ROWS)
    multiply(numbered, near_left, near_right, near_index, True)

    pl.when(jnp.logical_not(quick))(pass_on)
    for copy in to_onward:
        copy.wait_recv()
    unpack(far_pairs, far_left, far_right, 0)
    multiply(numbered[:3], far_left, far_right, far_index, False)

    def folded(c, s):
        even = acc[pl.ds(c * B, TILES), pl.ds(s * LANES, LANES)]
        odd = acc[pl.ds(c * B + TILES, TILES), pl.ds(s * LANES, LANES)]
        return jnp.where(low, even + swap(even), odd + swap(odd))

    for s in range(KC):
        part_out[s] = folded(1 - core, s)
    to_part = pltpu.make_async_remote_copy(
        part_out, part_in, send_sem.at[0], recv_sem.at[0], device_id=sibling, device_id_type=MESH
    )
    to_part.start()
    mine = [folded(core, s) for s in range(KC)]
    to_part.wait_recv()
    for s in range(KC):
        out[s] = mine[s] + part_in[s]
    for copy in (*to_relay, *to_onward, to_sib, to_part):
        copy.wait_send()


def local(n_wide, n_narrow, a_blocks, p_blocks, columns, aggregate, target):
    hbm = pl.BlockSpec(memory_space=pltpu.HBM)
    vmem = pltpu.VMEM
    smem = pltpu.SMEM
    operands = (columns.T, aggregate, target.T, p_blocks, jnp.transpose(a_blocks, (1, 0, 2)))
    result = pl.pallas_call(
        functools.partial(kernel, n_wide, n_narrow),
        out_shape=jax.ShapeDtypeStruct((KC, TILES, LANES), F32),
        in_specs=[hbm] * 5,
        out_specs=pl.BlockSpec(memory_space=pltpu.VMEM),
        scratch_shapes=[
            smem((K, ROWS), jnp.int32),
            smem((ROWS,), jnp.int32),
            smem((K, ROWS), jnp.int32),
            vmem((ROWS, B * B), BF16),
            vmem((K, ROWS, B * B), BF16),
            vmem((TILES * ROWS, LANES), F32),
            vmem((K * TILES * ROWS, LANES), F32),
            vmem((ROWS // 2 * B, LANES), F32),
            vmem((ROWS // 2, B, LANES), BF16),
            vmem((ROWS // 2, B, LANES), BF16),
            vmem((ROWS // 2, B, LANES), BF16),
            vmem((ROWS // 2, B, LANES), BF16),
            vmem((2 * ROWS + 1, B, LANES), BF16),
            vmem((2 * ROWS + 1, B, LANES), BF16),
            vmem((ROWS + 1, B, LANES), BF16),
            vmem((ROWS + 1, B, LANES), BF16),
            vmem((ROWS * len(PAIRS), B, LANES), BF16),
            vmem((GROUP, B, KC * LANES), BF16),
            vmem((LANES, LANES), F32),
            vmem((ROWS // 2, LANES, LANES), BF16),
            vmem((LANES, KC * LANES), F32),
            vmem((KC, TILES, LANES), F32),
            vmem((KC, TILES, LANES), F32),
            pltpu.SemaphoreType.DMA((5,)),
            pltpu.SemaphoreType.DMA((2 + 2 * CHUNKS,)),
            pltpu.SemaphoreType.DMA((2 + 2 * CHUNKS,)),
        ],
        compiler_params=pltpu.CompilerParams(
            collective_id=0, has_side_effects=True, vmem_limit_bytes=40 * 2**20
        ),
    )(*(pltpu.with_memory_space_constraint(value, pltpu.HBM) for value in operands))
    return result.reshape(1, KC, B * B)


def solution(mesh):
    placed = (
        P(("wide", "narrow"), None, None),
        P(("wide", "narrow"), None),
        P(("wide", "narrow"), None),
        P(("wide", "narrow")),
        P(("wide", "narrow"), None),
    )
    return jax.shard_map(
        functools.partial(local, mesh.shape["wide"], mesh.shape["narrow"]),
        mesh=mesh,
        in_specs=placed,
        out_specs=P(("wide", "narrow"), None, None),
        check_vma=False,
    )
```

```python
import functools

import jax
import jax.numpy as jnp
from jax import lax
from jax.experimental import pallas as pl
from jax.experimental.pallas import tpu as pltpu
from jax.sharding import PartitionSpec as P

B = 64
K = 7
KC = 7
ROWS = 16
TILES = 32
LANES = 128
PAIRS = ((1, 2), (3, 4), (5, 6), (0, None))
GROUP = 4
X_CHIPS = 4
CHUNKS = 4
F32 = jnp.float32
BF16 = jnp.bfloat16
MESH = pl.DeviceIdType.MESH


def swap(x):
    return pltpu.roll(x, B, 1)


def kernel(
    n_wide,
    n_narrow,
    cols_hbm,
    agg_hbm,
    targ_hbm,
    p_hbm,
    a_hbm,
    out,
    cols,
    agg,
    targ,
    p_raw,
    a_raw,
    p_f32,
    a_f32,
    pair_f32,
    own_pairs,
    sib_pairs,
    passing,
    far_pairs,
    near_left,
    near_right,
    far_left,
    far_right,
    blocks,
    y_all,
    pm_f32,
    pm_t,
    acc,
    part_out,
    part_in,
    load_sem,
    send_sem,
    recv_sem,
):
    total = n_wide * n_narrow
    me = lax.axis_index("wide") * n_narrow + lax.axis_index("narrow")
    core = me % 2

    def place(index):
        return (index // n_narrow, index % n_narrow)

    def far_of(index):
        return (index - 1 + 2 * (index % 2) + total) % total

    def relay_of(index, flipped):
        wide, narrow = index // n_narrow, index % n_narrow
        z_lo, x = wide // X_CHIPS, wide % X_CHIPS
        flip = (z_lo + index % 2 + flipped) % 2
        z_hi = narrow // 2 % 2
        wide = (z_lo + 1 - 2 * (z_lo % 2)) * X_CHIPS + x
        return wide * n_narrow + narrow + flip * (2 - 4 * z_hi)

    partner = far_of(me)
    source = relay_of(me, 1)
    quick = (me // n_narrow // X_CHIPS + core) % 2 == 1
    sibling = place(me + 1 - 2 * core)
    relay = place(relay_of(me, 0))
    onward = place(far_of(source))

    barrier = pltpu.get_barrier_semaphore()
    for other in (sibling, place(source), place(relay_of(partner, 0))):
        pl.semaphore_signal(barrier, inc=1, device_id=other, device_id_type=MESH)
    operands = ((p_hbm, p_raw), (a_hbm, a_raw), (cols_hbm, cols), (agg_hbm, agg), (targ_hbm, targ))
    loads = [
        pltpu.make_async_copy(source, dest, load_sem.at[n])
        for n, (source, dest) in enumerate(operands)
    ]
    for load in loads:
        load.start()

    low = lax.broadcasted_iota(jnp.int32, (TILES, LANES), 1) < B
    low_block = lax.broadcasted_iota(jnp.int32, (B, LANES), 1) < B
    low_row = low[:8]

    loads[0].wait()
    for t in range(TILES):
        p_f32[pl.ds(t * ROWS, ROWS), :] = p_raw[:, pl.ds(t * LANES, LANES)].astype(F32)
    for j in range(ROWS // 2):
        one = p_f32[pl.ds(j, TILES, stride=ROWS), :]
        two = p_f32[pl.ds(j + 8, TILES, stride=ROWS), :]
        pair_f32[pl.ds(j * B, TILES, stride=2), :] = jnp.where(low, one, swap(two))
        pair_f32[pl.ds(j * B + 1, TILES, stride=2), :] = jnp.where(low, swap(one), two)
    for j in range(ROWS // 2):
        own_pairs[j] = pair_f32[pl.ds(j * B, B), :].astype(BF16)

    def unpack(source, left, right, start):
        def one(j, carry):
            both = source[j].astype(F32)
            turned = swap(both)
            left[start + j] = jnp.where(low_block, both, 0.0).astype(BF16)
            right[start + j] = jnp.where(low_block, 0.0, turned).astype(BF16)
            left[start + j + 8] = jnp.where(low_block, turned, 0.0).astype(BF16)
            right[start + j + 8] = jnp.where(low_block, 0.0, both).astype(BF16)
            return carry

        lax.fori_loop(0, ROWS // 2, one, 0)

    unpack(own_pairs, near_left, near_right, 0)
    for ref, end in (
        (near_left, 2 * ROWS),
        (near_right, 2 * ROWS),
        (far_left, ROWS),
        (far_right, ROWS),
    ):
        ref[end] = jnp.zeros((B, LANES), BF16)

    loads[1].wait()

    def widen(k, carry):
        for t in range(TILES):
            a_f32[pl.ds(k * TILES * ROWS + t * ROWS, ROWS), :] = a_raw[
                k, :, pl.ds(t * LANES, LANES)
            ].astype(F32)
        return carry

    lax.fori_loop(0, K, widen, 0)

    def arrange(i, carry):
        for n, (k, other) in enumerate(PAIRS):
            one = a_f32[pl.ds(k * TILES * ROWS + i, TILES, stride=ROWS), :]
            if other is None:
                even = jnp.where(low, one, 0.0)
                odd = jnp.where(low, swap(one), 0.0)
            else:
                two = a_f32[pl.ds(other * TILES * ROWS + i, TILES, stride=ROWS), :]
                even = jnp.where(low, one, swap(two))
                odd = jnp.where(low, swap(one), two)
            blocks[i * len(PAIRS) + n] = jnp.concatenate([even, odd], axis=0).astype(BF16)
        return carry

    lax.fori_loop(0, ROWS, arrange, 0)

    for load in loads[2:]:
        load.wait()
    first = me - core

    def transpose(pair, carry):
        halves = []
        for i in (2 * pair, 2 * pair + 1):
            x = p_f32[pl.ds(i, TILES, stride=ROWS), :]
            y = swap(x)
            keep = [jnp.where(agg[i] == first + c, 1.0, 0.0) for c in range(2)]
            halves.append(jnp.where(low, x * keep[0], y * keep[1]))
            halves.append(jnp.where(low, y * keep[0], x * keep[1]))
        pm_f32[...] = jnp.concatenate(halves, axis=0).T
        rows = [pm_f32[pl.ds(c * B + h, TILES, stride=2), :] for c in range(2) for h in range(2)]
        pm_t[pair] = jnp.concatenate(rows, axis=0).astype(BF16)
        return carry

    lax.fori_loop(0, ROWS // 2, transpose, 0)

    pl.semaphore_wait(barrier, 3)
    step = ROWS // 2 // CHUNKS
    chunks = [pl.ds(n * step, step) for n in range(CHUNKS)]
    to_relay = [
        pltpu.make_async_remote_copy(
            own_pairs.at[chunk],
            passing.at[chunk],
            send_sem.at[2 + n],
            recv_sem.at[2 + n],
            device_id=relay,
            device_id_type=MESH,
        )
        for n, chunk in enumerate(chunks)
    ]
    to_onward = [
        pltpu.make_async_remote_copy(
            passing.at[chunk],
            far_pairs.at[chunk],
            send_sem.at[2 + CHUNKS + n],
            recv_sem.at[2 + CHUNKS + n],
            device_id=onward,
            device_id_type=MESH,
        )
        for n, chunk in enumerate(chunks)
    ]
    to_sib = pltpu.make_async_remote_copy(
        own_pairs, sib_pairs, send_sem.at[1], recv_sem.at[1], device_id=sibling, device_id_type=MESH
    )
    for copy in to_relay:
        copy.start()
    to_sib.start()

    def pass_on():
        for n in range(CHUNKS):
            to_relay[n].wait_recv()
            to_onward[n].start()

    root = (me - 1) * ROWS

    def near_index(at):
        plane, at = at // ROWS, at % ROWS
        return jnp.where(plane == 1, at, jnp.where(plane == 2 - 2 * core, at + ROWS, 2 * ROWS))

    def far_index(at):
        plane, at = at // ROWS, at % ROWS
        return jnp.where(plane == 2 * core, at, ROWS)

    def multiply(pairs, left, right, index_of, initial):
        def group(g, carry):
            for r in range(GROUP):
                i = g * GROUP + r
                applied, slots = [], []
                for n, (k, other) in pairs:
                    above = left[index_of(cols[k, i] - root)]
                    slot = jnp.full((8, LANES), targ[k, i], jnp.int32)
                    if other is None:
                        below = jnp.zeros((B, LANES), BF16)
                    else:
                        below = right[index_of(cols[other, i] - root)]
                        slot = jnp.where(low_row, slot, targ[other, i])
                    applied.append(
                        jnp.dot(
                            blocks[i * len(PAIRS) + n],
                            jnp.concatenate([above, below], axis=0),
                            preferred_element_type=F32,
                        )
                    )
                    slots.append(slot)
                for s in range(KC):
                    summed = None
                    for value, slot in zip(applied, slots):
                        mask = jnp.concatenate([jnp.where(slot == s, 1.0, 0.0)] * 8, axis=0)
                        term = value * mask
                        summed = term if summed is None else summed + term
                    y_all[r, :, pl.ds(s * LANES, LANES)] = summed.astype(BF16)
            weights = jnp.concatenate(
                [pm_t[g * (GROUP // 2) + n] for n in range(GROUP // 2)], axis=1
            )
            partial = jnp.dot(
                weights,
                y_all[...].reshape(GROUP * B, KC * LANES),
                preferred_element_type=F32,
            )
            acc[...] += partial
            return carry

        if initial:
            acc[...] = jnp.zeros_like(acc)
        lax.fori_loop(0, ROWS // GROUP, group, 0)

    numbered = list(enumerate(PAIRS))
    to_sib.wait_recv()
    unpack(sib_pairs, near_left, near_right, ROWS)
    pl.when(quick)(pass_on)
    multiply(numbered, near_left, near_right, near_index, True)

    pl.when(jnp.logical_not(quick))(pass_on)
    for copy in to_onward:
        copy.wait_recv()
    unpack(far_pairs, far_left, far_right, 0)
    multiply(numbered[:3], far_left, far_right, far_index, False)

    def folded(c, s):
        even = acc[pl.ds(c * B, TILES), pl.ds(s * LANES, LANES)]
        odd = acc[pl.ds(c * B + TILES, TILES), pl.ds(s * LANES, LANES)]
        return jnp.where(low, even + swap(even), odd + swap(odd))

    for s in range(KC):
        part_out[s] = folded(1 - core, s)
    to_part = pltpu.make_async_remote_copy(
        part_out, part_in, send_sem.at[0], recv_sem.at[0], device_id=sibling, device_id_type=MESH
    )
    to_part.start()
    mine = [folded(core, s) for s in range(KC)]
    to_part.wait_recv()
    for s in range(KC):
        out[s] = mine[s] + part_in[s]
    for copy in (*to_relay, *to_onward, to_sib, to_part):
        copy.wait_send()


def local(n_wide, n_narrow, a_blocks, p_blocks, columns, aggregate, target):
    hbm = pl.BlockSpec(memory_space=pltpu.HBM)
    vmem = pltpu.VMEM
    smem = pltpu.SMEM
    operands = (columns.T, aggregate, target.T, p_blocks, jnp.transpose(a_blocks, (1, 0, 2)))
    result = pl.pallas_call(
        functools.partial(kernel, n_wide, n_narrow),
        out_shape=jax.ShapeDtypeStruct((KC, TILES, LANES), F32),
        in_specs=[hbm] * 5,
        out_specs=pl.BlockSpec(memory_space=pltpu.VMEM),
        scratch_shapes=[
            smem((K, ROWS), jnp.int32),
            smem((ROWS,), jnp.int32),
            smem((K, ROWS), jnp.int32),
            vmem((ROWS, B * B), BF16),
            vmem((K, ROWS, B * B), BF16),
            vmem((TILES * ROWS, LANES), F32),
            vmem((K * TILES * ROWS, LANES), F32),
            vmem((ROWS // 2 * B, LANES), F32),
            vmem((ROWS // 2, B, LANES), BF16),
            vmem((ROWS // 2, B, LANES), BF16),
            vmem((ROWS // 2, B, LANES), BF16),
            vmem((ROWS // 2, B, LANES), BF16),
            vmem((2 * ROWS + 1, B, LANES), BF16),
            vmem((2 * ROWS + 1, B, LANES), BF16),
            vmem((ROWS + 1, B, LANES), BF16),
            vmem((ROWS + 1, B, LANES), BF16),
            vmem((ROWS * len(PAIRS), B, LANES), BF16),
            vmem((GROUP, B, KC * LANES), BF16),
            vmem((LANES, LANES), F32),
            vmem((ROWS // 2, LANES, LANES), BF16),
            vmem((LANES, KC * LANES), F32),
            vmem((KC, TILES, LANES), F32),
            vmem((KC, TILES, LANES), F32),
            pltpu.SemaphoreType.DMA((5,)),
            pltpu.SemaphoreType.DMA((2 + 2 * CHUNKS,)),
            pltpu.SemaphoreType.DMA((2 + 2 * CHUNKS,)),
        ],
        compiler_params=pltpu.CompilerParams(
            collective_id=0, has_side_effects=True, vmem_limit_bytes=40 * 2**20
        ),
    )(*(pltpu.with_memory_space_constraint(value, pltpu.HBM) for value in operands))
    return result.reshape(1, KC, B * B)


def solution(mesh):
    placed = (
        P(("wide", "narrow"), None, None),
        P(("wide", "narrow"), None),
        P(("wide", "narrow"), None),
        P(("wide", "narrow")),
        P(("wide", "narrow"), None),
    )
    return jax.shard_map(
        functools.partial(local, mesh.shape["wide"], mesh.shape["narrow"]),
        mesh=mesh,
        in_specs=placed,
        out_specs=P(("wide", "narrow"), None, None),
        check_vma=False,
    )
```

```python
import functools

import jax
import jax.numpy as jnp
from jax import lax
from jax.experimental import pallas as pl
from jax.experimental.pallas import tpu as pltpu
from jax.sharding import PartitionSpec as P

B = 64
K = 7
KC = 7
ROWS = 16
TILES = 32
LANES = 128
HALF = 256
PAIRS = ((1, 2), (3, 4), (5, 6), (0, None))
GROUP = 4
X_CHIPS = 4
CHUNKS = 4
F32 = jnp.float32
BF16 = jnp.bfloat16
MESH = pl.DeviceIdType.MESH


def swap(x):
    return pltpu.roll(x, B, 1)


def kernel(
    n_wide,
    n_narrow,
    cols_hbm,
    agg_hbm,
    targ_hbm,
    p_hbm,
    a_hbm,
    out,
    cols,
    agg,
    targ,
    p_raw,
    a_raw,
    p_f32,
    own_pairs,
    sib_pairs,
    passing,
    far_pairs,
    near_left,
    near_right,
    far_left,
    far_right,
    blocks,
    y_all,
    masked,
    masked_t,
    acc,
    part_out,
    part_in,
    load_sem,
    send_sem,
    recv_sem,
):
    total = n_wide * n_narrow
    me = lax.axis_index("wide") * n_narrow + lax.axis_index("narrow")
    core = me % 2

    def place(index):
        return (index // n_narrow, index % n_narrow)

    def far_of(index):
        return (index - 1 + 2 * (index % 2) + total) % total

    def relay_of(index, flipped):
        wide, narrow = index // n_narrow, index % n_narrow
        z_lo, x = wide // X_CHIPS, wide % X_CHIPS
        flip = (z_lo + index % 2 + flipped) % 2
        z_hi = narrow // 2 % 2
        wide = (z_lo + 1 - 2 * (z_lo % 2)) * X_CHIPS + x
        return wide * n_narrow + narrow + flip * (2 - 4 * z_hi)

    partner = far_of(me)
    source = relay_of(me, 1)
    quick = (me // n_narrow // X_CHIPS + core) % 2 == 1
    sibling = place(me + 1 - 2 * core)
    relay = place(relay_of(me, 0))
    onward = place(far_of(source))

    barrier = pltpu.get_barrier_semaphore()
    for other in (sibling, place(source), place(relay_of(partner, 0))):
        pl.semaphore_signal(barrier, inc=1, device_id=other, device_id_type=MESH)
    operands = ((p_hbm, p_raw), (a_hbm, a_raw), (cols_hbm, cols), (agg_hbm, agg), (targ_hbm, targ))
    loads = [
        pltpu.make_async_copy(source, dest, load_sem.at[n])
        for n, (source, dest) in enumerate(operands)
    ]
    for load in loads:
        load.start()

    def iota(rows, columns):
        shape = (rows, columns)
        return (lax.broadcasted_iota(jnp.int32, shape, 0), lax.broadcasted_iota(jnp.int32, shape, 1))

    def ones_where(condition):
        return jnp.where(condition, 1.0, 0.0).astype(BF16)

    low = iota(ROWS, LANES)[1] < B
    low_block = iota(B, LANES)[1] < B
    low_tiles = iota(TILES, LANES)[1] < B
    low_row = low[:8]

    row, column = iota(HALF, HALF)
    turn = ones_where((row >> 4 == (column & 15)) & ((row & 15) == column >> 4))
    row, column = iota(2 * HALF, HALF)
    turn_twice = ones_where((row >> 5 == (column & 15)) & ((row >> 1 & 15) == column >> 4))

    def stack(tile):
        return jnp.concatenate([tile(t) for t in range(ROWS)], axis=0)

    loads[0].wait()
    flat = jnp.concatenate(
        [
            stack(lambda t, half=half: p_raw[:, pl.ds((half * ROWS + t) * LANES, LANES)])
            for half in range(2)
        ],
        axis=1,
    )
    doubled = jnp.dot(turn_twice, flat, preferred_element_type=F32)
    first_row = (iota(TILES, LANES)[0] & 1) == 0
    for j in range(ROWS // 2):
        for half in range(2):
            lanes = slice(half * LANES, (half + 1) * LANES)
            one = doubled[j * TILES : (j + 1) * TILES, lanes]
            two = doubled[(j + 8) * TILES : (j + 9) * TILES, lanes]
            left = jnp.where(first_row, one, swap(one))
            right = jnp.where(first_row, swap(two), two)
            own_pairs[j, pl.ds(half * TILES, TILES), :] = jnp.where(low_tiles, left, right).astype(BF16)

    pl.semaphore_wait(barrier, 3)
    step = ROWS // 2 // CHUNKS
    chunks = [pl.ds(n * step, step) for n in range(CHUNKS)]
    to_relay = [
        pltpu.make_async_remote_copy(
            own_pairs.at[chunk],
            passing.at[chunk],
            send_sem.at[2 + n],
            recv_sem.at[2 + n],
            device_id=relay,
            device_id_type=MESH,
        )
        for n, chunk in enumerate(chunks)
    ]
    to_onward = [
        pltpu.make_async_remote_copy(
            passing.at[chunk],
            far_pairs.at[chunk],
            send_sem.at[2 + CHUNKS + n],
            recv_sem.at[2 + CHUNKS + n],
            device_id=onward,
            device_id_type=MESH,
        )
        for n, chunk in enumerate(chunks)
    ]
    to_sib = pltpu.make_async_remote_copy(
        own_pairs, sib_pairs, send_sem.at[1], recv_sem.at[1], device_id=sibling, device_id_type=MESH
    )
    for copy in to_relay:
        copy.start()
    to_sib.start()

    def pass_on():
        for n in range(CHUNKS):
            to_relay[n].wait_recv()
            to_onward[n].start()

    loads[1].wait()
    for n, (k, other) in enumerate(PAIRS):
        for half in range(2):

            def tile(t, which, half=half):
                return a_raw[which, :, pl.ds((half * ROWS + t) * LANES, LANES)]

            def side(h, t, k=k, other=other, tile=tile):
                one = tile(t, k)[:, h * B : (h + 1) * B]
                two = jnp.zeros_like(one) if other is None else tile(t, other)[:, h * B : (h + 1) * B]
                return jnp.concatenate([one, two], axis=1)

            both = jnp.concatenate(
                [stack(functools.partial(side, h)) for h in range(2)], axis=1
            )
            turned = jnp.dot(turn, both, preferred_element_type=F32).astype(BF16)
            for h in range(2):
                blocks[n, 2 * h + half] = turned[:, h * LANES : (h + 1) * LANES]

    def unpack(source, left, right, start):
        def one(j, carry):
            both = source[j].astype(F32)
            turned = swap(both)
            left[start + j] = jnp.where(low_block, both, 0.0).astype(BF16)
            right[start + j] = jnp.where(low_block, 0.0, turned).astype(BF16)
            left[start + j + 8] = jnp.where(low_block, turned, 0.0).astype(BF16)
            right[start + j + 8] = jnp.where(low_block, 0.0, both).astype(BF16)
            return carry

        lax.fori_loop(0, ROWS // 2, one, 0, unroll=2)

    def clear(left, right, start):
        def one(j, carry):
            left[start + j] = jnp.zeros((B, LANES), BF16)
            right[start + j] = jnp.zeros((B, LANES), BF16)
            return carry

        lax.fori_loop(0, ROWS, one, 0, unroll=4)

    far_start = 2 * ROWS * core
    sib_start = 2 * ROWS - far_start
    clear(near_left, near_right, far_start)
    clear(far_left, far_right, ROWS)
    clear(far_left, far_right, sib_start)
    unpack(own_pairs, near_left, near_right, ROWS)

    for load in loads[2:]:
        load.wait()
    first = me - core
    together = jnp.dot(turn, flat, preferred_element_type=F32)
    p_f32[0] = together[:, :LANES]
    p_f32[1] = together[:, LANES:]

    def mask(i, carry):
        keep = [jnp.where(agg[i] == first + c, 1.0, 0.0) for c in range(2)]
        for half in range(2):
            x = p_f32[half, pl.ds(pl.multiple_of(i * ROWS, ROWS), ROWS), :]
            y = swap(x)
            masked[i, pl.ds(half * ROWS, ROWS), :] = jnp.where(low, x * keep[0], y * keep[1]).astype(BF16)
            masked[i, pl.ds(TILES + half * ROWS, ROWS), :] = jnp.where(
                low, y * keep[0], x * keep[1]
            ).astype(BF16)
        return carry

    lax.fori_loop(0, ROWS, mask, 0, unroll=4)
    row, column = iota(LANES, LANES)
    order = ones_where(column == (row >> 6 << 6) + 2 * (row & 31) + (row >> 5 & 1))
    masked_t[...] = lax.dot_general(
        order,
        masked[...].reshape(ROWS * B, LANES),
        (((1,), (1,)), ((), ())),
        preferred_element_type=F32,
    ).astype(BF16)

    root = (me - 1) * ROWS

    def entry(k, i):
        return jnp.clip(cols[k, i] - root, 0, 3 * ROWS - 1)

    def multiply(pairs, left, right):
        def group(g, carry):
            for r in range(GROUP):
                i = g * GROUP + r
                applied, slots = [], []
                for n, (k, other) in pairs:
                    above = left[entry(k, i)]
                    slot = jnp.full((8, LANES), targ[k, i], jnp.int32)
                    if other is None:
                        below = jnp.zeros((B, LANES), BF16)
                    else:
                        below = right[entry(other, i)]
                        slot = jnp.where(low_row, slot, targ[other, i])
                    rows = pl.ds(pl.multiple_of(i * ROWS, ROWS), ROWS)
                    applied.append(
                        jnp.dot(
                            jnp.concatenate([blocks[n, q, rows, :] for q in range(4)], axis=0),
                            jnp.concatenate([above, below], axis=0),
                            preferred_element_type=F32,
                        )
                    )
                    slots.append(slot)
                for s in range(KC):
                    summed = None
                    for value, slot in zip(applied, slots):
                        keep = jnp.concatenate([jnp.where(slot == s, 1.0, 0.0)] * 8, axis=0)
                        term = value * keep
                        summed = term if summed is None else summed + term
                    y_all[i, :, pl.ds(s * LANES, LANES)] = summed.astype(BF16)
            return carry

        lax.fori_loop(0, ROWS // GROUP, group, 0)
        return jnp.dot(
            masked_t[...],
            y_all[...].reshape(ROWS * B, KC * LANES),
            preferred_element_type=F32,
        )

    numbered = list(enumerate(PAIRS))
    to_sib.wait_recv()
    unpack(sib_pairs, near_left, near_right, sib_start)
    pl.when(quick)(pass_on)
    acc[...] = multiply(numbered, near_left, near_right)

    pl.when(jnp.logical_not(quick))(pass_on)
    for copy in to_onward:
        copy.wait_recv()
    unpack(far_pairs, far_left, far_right, far_start)
    acc[...] += multiply(numbered[:3], far_left, far_right)

    def folded(c, s):
        even = acc[pl.ds(c * B, TILES), pl.ds(s * LANES, LANES)]
        odd = acc[pl.ds(c * B + TILES, TILES), pl.ds(s * LANES, LANES)]
        return jnp.where(low_tiles, even + swap(even), odd + swap(odd))

    for s in range(KC):
        part_out[s] = folded(1 - core, s)
    to_part = pltpu.make_async_remote_copy(
        part_out, part_in, send_sem.at[0], recv_sem.at[0], device_id=sibling, device_id_type=MESH
    )
    to_part.start()
    mine = [folded(core, s) for s in range(KC)]
    to_part.wait_recv()
    for s in range(KC):
        out[s] = mine[s] + part_in[s]
    for copy in (*to_relay, *to_onward, to_sib, to_part):
        copy.wait_send()


def local(n_wide, n_narrow, a_blocks, p_blocks, columns, aggregate, target):
    hbm = pl.BlockSpec(memory_space=pltpu.HBM)
    vmem = pltpu.VMEM
    smem = pltpu.SMEM
    operands = (columns.T, aggregate, target.T, p_blocks, jnp.transpose(a_blocks, (1, 0, 2)))
    result = pl.pallas_call(
        functools.partial(kernel, n_wide, n_narrow),
        out_shape=jax.ShapeDtypeStruct((KC, TILES, LANES), F32),
        in_specs=[hbm] * 5,
        out_specs=pl.BlockSpec(memory_space=pltpu.VMEM),
        scratch_shapes=[
            smem((K, ROWS), jnp.int32),
            smem((ROWS,), jnp.int32),
            smem((K, ROWS), jnp.int32),
            vmem((ROWS, B * B), BF16),
            vmem((K, ROWS, B * B), BF16),
            vmem((2, HALF, LANES), F32),
            vmem((ROWS // 2, B, LANES), BF16),
            vmem((ROWS // 2, B, LANES), BF16),
            vmem((ROWS // 2, B, LANES), BF16),
            vmem((ROWS // 2, B, LANES), BF16),
            vmem((3 * ROWS, B, LANES), BF16),
            vmem((3 * ROWS, B, LANES), BF16),
            vmem((3 * ROWS, B, LANES), BF16),
            vmem((3 * ROWS, B, LANES), BF16),
            vmem((len(PAIRS), 4, HALF, LANES), BF16),
            vmem((ROWS, B, KC * LANES), BF16),
            vmem((ROWS, B, LANES), BF16),
            vmem((LANES, ROWS * B), BF16),
            vmem((LANES, KC * LANES), F32),
            vmem((KC, TILES, LANES), F32),
            vmem((KC, TILES, LANES), F32),
            pltpu.SemaphoreType.DMA((5,)),
            pltpu.SemaphoreType.DMA((2 + 2 * CHUNKS,)),
            pltpu.SemaphoreType.DMA((2 + 2 * CHUNKS,)),
        ],
        compiler_params=pltpu.CompilerParams(
            collective_id=0, has_side_effects=True, vmem_limit_bytes=40 * 2**20
        ),
    )(*(pltpu.with_memory_space_constraint(value, pltpu.HBM) for value in operands))
    return result.reshape(1, KC, B * B)


def solution(mesh):
    placed = (
        P(("wide", "narrow"), None, None),
        P(("wide", "narrow"), None),
        P(("wide", "narrow"), None),
        P(("wide", "narrow")),
        P(("wide", "narrow"), None),
    )
    return jax.shard_map(
        functools.partial(local, mesh.shape["wide"], mesh.shape["narrow"]),
        mesh=mesh,
        in_specs=placed,
        out_specs=P(("wide", "narrow"), None, None),
        check_vma=False,
    )
```

```python
import functools

import jax
import jax.numpy as jnp
from jax import lax
from jax.experimental import pallas as pl
from jax.experimental.pallas import tpu as pltpu
from jax.sharding import PartitionSpec as P

B = 64
K = 7
KC = 7
ROWS = 16
TILES = 32
LANES = 128
HALF = 256
PAIRS = ((1, 2), (3, 4), (5, 6), (0, None))
GROUP = 4
X_CHIPS = 4
CHUNKS = 4
F32 = jnp.float32
BF16 = jnp.bfloat16
MESH = pl.DeviceIdType.MESH


def swap(x):
    return pltpu.roll(x, B, 1)


def kernel(
    n_wide,
    n_narrow,
    cols_hbm,
    agg_hbm,
    targ_hbm,
    p_hbm,
    a_hbm,
    out,
    cols,
    agg,
    targ,
    p_raw,
    a_raw,
    p_f32,
    own_pairs,
    sib_pairs,
    passing,
    far_pairs,
    near_left,
    near_right,
    far_left,
    far_right,
    blocks,
    y_all,
    masked,
    masked_t,
    acc,
    part_out,
    part_in,
    load_sem,
    send_sem,
    recv_sem,
):
    total = n_wide * n_narrow
    me = lax.axis_index("wide") * n_narrow + lax.axis_index("narrow")
    core = me % 2

    def place(index):
        return (index // n_narrow, index % n_narrow)

    def far_of(index):
        return (index - 1 + 2 * (index % 2) + total) % total

    def up(index, chips):
        wide, narrow = index // n_narrow, index % n_narrow
        z_lo, x = wide // X_CHIPS, wide % X_CHIPS
        z_hi = narrow // 2 % 2
        z = (z_hi * z_run + z_lo + chips + 2 * z_run) % (2 * z_run)
        return (z % z_run * X_CHIPS + x) * n_narrow + narrow + 2 * (z // z_run - z_hi)

    z_run = n_wide // X_CHIPS
    way = 1 - 2 * core
    partner = far_of(me)
    source = up(me, -way)
    sibling = place(me + 1 - 2 * core)
    relay = place(up(me, way))
    onward = place(far_of(source))

    barrier = pltpu.get_barrier_semaphore()
    for other in (sibling, place(source), place(up(partner, -way))):
        pl.semaphore_signal(barrier, inc=1, device_id=other, device_id_type=MESH)
    operands = ((p_hbm, p_raw), (a_hbm, a_raw), (cols_hbm, cols), (agg_hbm, agg), (targ_hbm, targ))
    loads = [
        pltpu.make_async_copy(source, dest, load_sem.at[n])
        for n, (source, dest) in enumerate(operands)
    ]
    for load in loads:
        load.start()

    def iota(rows, columns):
        shape = (rows, columns)
        return (lax.broadcasted_iota(jnp.int32, shape, 0), lax.broadcasted_iota(jnp.int32, shape, 1))

    def ones_where(condition):
        return jnp.where(condition, 1.0, 0.0).astype(BF16)

    low = iota(ROWS, LANES)[1] < B
    low_block = iota(B, LANES)[1] < B
    low_tiles = iota(TILES, LANES)[1] < B
    low_row = low[:8]

    row, column = iota(HALF, HALF)
    turn = ones_where((row >> 4 == (column & 15)) & ((row & 15) == column >> 4))
    row, column = iota(2 * HALF, HALF)
    turn_twice = ones_where((row >> 5 == (column & 15)) & ((row >> 1 & 15) == column >> 4))

    def stack(tile):
        return jnp.concatenate([tile(t) for t in range(ROWS)], axis=0)

    loads[0].wait()
    flat = jnp.concatenate(
        [
            stack(lambda t, half=half: p_raw[:, pl.ds((half * ROWS + t) * LANES, LANES)])
            for half in range(2)
        ],
        axis=1,
    )
    doubled = jnp.dot(turn_twice, flat, preferred_element_type=F32)
    pl.semaphore_wait(barrier, 3)
    step = ROWS // 2 // CHUNKS
    chunks = [pl.ds(n * step, step) for n in range(CHUNKS)]
    to_relay = [
        pltpu.make_async_remote_copy(
            own_pairs.at[chunk],
            passing.at[chunk],
            send_sem.at[2 + n],
            recv_sem.at[2 + n],
            device_id=relay,
            device_id_type=MESH,
        )
        for n, chunk in enumerate(chunks)
    ]
    to_onward = [
        pltpu.make_async_remote_copy(
            passing.at[chunk],
            far_pairs.at[chunk],
            send_sem.at[2 + CHUNKS + n],
            recv_sem.at[2 + CHUNKS + n],
            device_id=onward,
            device_id_type=MESH,
        )
        for n, chunk in enumerate(chunks)
    ]
    to_sib = pltpu.make_async_remote_copy(
        own_pairs, sib_pairs, send_sem.at[1], recv_sem.at[1], device_id=sibling, device_id_type=MESH
    )
    first_row = (iota(TILES, LANES)[0] & 1) == 0
    for j in range(ROWS // 2):
        for half in range(2):
            lanes = slice(half * LANES, (half + 1) * LANES)
            one = doubled[j * TILES : (j + 1) * TILES, lanes]
            two = doubled[(j + 8) * TILES : (j + 9) * TILES, lanes]
            left = jnp.where(first_row, one, swap(one))
            right = jnp.where(first_row, swap(two), two)
            own_pairs[j, pl.ds(half * TILES, TILES), :] = jnp.where(low_tiles, left, right).astype(BF16)
        if (j + 1) % step == 0:
            to_relay[j // step].start()
    to_sib.start()

    loads[1].wait()
    for n, (k, other) in enumerate(PAIRS):
        for half in range(2):

            def tile(t, which, half=half):
                return a_raw[which, :, pl.ds((half * ROWS + t) * LANES, LANES)]

            def side(h, t, k=k, other=other, tile=tile):
                one = tile(t, k)[:, h * B : (h + 1) * B]
                two = jnp.zeros_like(one) if other is None else tile(t, other)[:, h * B : (h + 1) * B]
                return jnp.concatenate([one, two], axis=1)

            both = jnp.concatenate(
                [stack(functools.partial(side, h)) for h in range(2)], axis=1
            )
            turned = jnp.dot(turn, both, preferred_element_type=F32).astype(BF16)
            for h in range(2):
                blocks[n, 2 * h + half] = turned[:, h * LANES : (h + 1) * LANES]
        to_relay[n].wait_recv()
        to_onward[n].start()

    def unpack(source, left, right, start, begin=0, end=ROWS // 2):
        def one(j, carry):
            both = source[j].astype(F32)
            turned = swap(both)
            left[start + j] = jnp.where(low_block, both, 0.0).astype(BF16)
            right[start + j] = jnp.where(low_block, 0.0, turned).astype(BF16)
            left[start + j + 8] = jnp.where(low_block, turned, 0.0).astype(BF16)
            right[start + j + 8] = jnp.where(low_block, 0.0, both).astype(BF16)
            return carry

        lax.fori_loop(begin, end, one, 0, unroll=2)

    def clear(left, right, start):
        def one(j, carry):
            left[start + j] = jnp.zeros((B, LANES), BF16)
            right[start + j] = jnp.zeros((B, LANES), BF16)
            return carry

        lax.fori_loop(0, ROWS, one, 0, unroll=4)

    far_start = 2 * ROWS * core
    sib_start = 2 * ROWS - far_start
    clear(near_left, near_right, far_start)
    clear(far_left, far_right, ROWS)
    clear(far_left, far_right, sib_start)
    unpack(own_pairs, near_left, near_right, ROWS)

    for load in loads[2:]:
        load.wait()
    first = me - core
    together = jnp.dot(turn, flat, preferred_element_type=F32)
    p_f32[0] = together[:, :LANES]
    p_f32[1] = together[:, LANES:]

    def mask(i, carry):
        keep = [jnp.where(agg[i] == first + c, 1.0, 0.0) for c in range(2)]
        for half in range(2):
            x = p_f32[half, pl.ds(pl.multiple_of(i * ROWS, ROWS), ROWS), :]
            y = swap(x)
            masked[i, pl.ds(half * ROWS, ROWS), :] = jnp.where(low, x * keep[0], y * keep[1]).astype(BF16)
            masked[i, pl.ds(TILES + half * ROWS, ROWS), :] = jnp.where(
                low, y * keep[0], x * keep[1]
            ).astype(BF16)
        return carry

    lax.fori_loop(0, ROWS, mask, 0, unroll=4)
    row, column = iota(LANES, LANES)
    order = ones_where(column == (row >> 6 << 6) + 2 * (row & 31) + (row >> 5 & 1))
    masked_t[...] = lax.dot_general(
        order,
        masked[...].reshape(ROWS * B, LANES),
        (((1,), (1,)), ((), ())),
        preferred_element_type=F32,
    ).astype(BF16)

    root = (me - 1) * ROWS

    def entry(k, i):
        return jnp.clip(cols[k, i] - root, 0, 3 * ROWS - 1)

    def multiply(pairs, left, right):
        def group(g, carry):
            for r in range(GROUP):
                i = g * GROUP + r
                applied, slots = [], []
                for n, (k, other) in pairs:
                    above = left[entry(k, i)]
                    slot = jnp.full((8, LANES), targ[k, i], jnp.int32)
                    if other is None:
                        below = jnp.zeros((B, LANES), BF16)
                    else:
                        below = right[entry(other, i)]
                        slot = jnp.where(low_row, slot, targ[other, i])
                    rows = pl.ds(pl.multiple_of(i * ROWS, ROWS), ROWS)
                    applied.append(
                        jnp.dot(
                            jnp.concatenate([blocks[n, q, rows, :] for q in range(4)], axis=0),
                            jnp.concatenate([above, below], axis=0),
                            preferred_element_type=F32,
                        )
                    )
                    slots.append(slot)
                for s in range(KC):
                    summed = None
                    for value, slot in zip(applied, slots):
                        keep = jnp.concatenate([jnp.where(slot == s, 1.0, 0.0)] * 8, axis=0)
                        term = value * keep
                        summed = term if summed is None else summed + term
                    y_all[i, :, pl.ds(s * LANES, LANES)] = summed.astype(BF16)
            return carry

        lax.fori_loop(0, ROWS // GROUP, group, 0)
        return jnp.dot(
            masked_t[...],
            y_all[...].reshape(ROWS * B, KC * LANES),
            preferred_element_type=F32,
        )

    numbered = list(enumerate(PAIRS))
    to_sib.wait_recv()
    unpack(sib_pairs, near_left, near_right, sib_start)
    acc[...] = multiply(numbered, near_left, near_right)

    for n, copy in enumerate(to_onward):
        copy.wait_recv()
        unpack(far_pairs, far_left, far_right, far_start, n * step, (n + 1) * step)
    acc[...] += multiply(numbered[:3], far_left, far_right)

    def folded(c, s):
        even = acc[pl.ds(c * B, TILES), pl.ds(s * LANES, LANES)]
        odd = acc[pl.ds(c * B + TILES, TILES), pl.ds(s * LANES, LANES)]
        return jnp.where(low_tiles, even + swap(even), odd + swap(odd))

    for s in range(KC):
        part_out[s] = folded(1 - core, s)
    to_part = pltpu.make_async_remote_copy(
        part_out, part_in, send_sem.at[0], recv_sem.at[0], device_id=sibling, device_id_type=MESH
    )
    to_part.start()
    mine = [folded(core, s) for s in range(KC)]
    to_part.wait_recv()
    for s in range(KC):
        out[s] = mine[s] + part_in[s]
    for copy in (*to_relay, *to_onward, to_sib, to_part):
        copy.wait_send()


def local(n_wide, n_narrow, a_blocks, p_blocks, columns, aggregate, target):
    hbm = pl.BlockSpec(memory_space=pltpu.HBM)
    vmem = pltpu.VMEM
    smem = pltpu.SMEM
    operands = (columns.T, aggregate, target.T, p_blocks, jnp.transpose(a_blocks, (1, 0, 2)))
    result = pl.pallas_call(
        functools.partial(kernel, n_wide, n_narrow),
        out_shape=jax.ShapeDtypeStruct((KC, TILES, LANES), F32),
        in_specs=[hbm] * 5,
        out_specs=pl.BlockSpec(memory_space=pltpu.VMEM),
        scratch_shapes=[
            smem((K, ROWS), jnp.int32),
            smem((ROWS,), jnp.int32),
            smem((K, ROWS), jnp.int32),
            vmem((ROWS, B * B), BF16),
            vmem((K, ROWS, B * B), BF16),
            vmem((2, HALF, LANES), F32),
            vmem((ROWS // 2, B, LANES), BF16),
            vmem((ROWS // 2, B, LANES), BF16),
            vmem((ROWS // 2, B, LANES), BF16),
            vmem((ROWS // 2, B, LANES), BF16),
            vmem((3 * ROWS, B, LANES), BF16),
            vmem((3 * ROWS, B, LANES), BF16),
            vmem((3 * ROWS, B, LANES), BF16),
            vmem((3 * ROWS, B, LANES), BF16),
            vmem((len(PAIRS), 4, HALF, LANES), BF16),
            vmem((ROWS, B, KC * LANES), BF16),
            vmem((ROWS, B, LANES), BF16),
            vmem((LANES, ROWS * B), BF16),
            vmem((LANES, KC * LANES), F32),
            vmem((KC, TILES, LANES), F32),
            vmem((KC, TILES, LANES), F32),
            pltpu.SemaphoreType.DMA((5,)),
            pltpu.SemaphoreType.DMA((2 + 2 * CHUNKS,)),
            pltpu.SemaphoreType.DMA((2 + 2 * CHUNKS,)),
        ],
        compiler_params=pltpu.CompilerParams(
            collective_id=0, has_side_effects=True, vmem_limit_bytes=40 * 2**20
        ),
    )(*(pltpu.with_memory_space_constraint(value, pltpu.HBM) for value in operands))
    return result.reshape(1, KC, B * B)


def solution(mesh):
    placed = (
        P(("wide", "narrow"), None, None),
        P(("wide", "narrow"), None),
        P(("wide", "narrow"), None),
        P(("wide", "narrow")),
        P(("wide", "narrow"), None),
    )
    return jax.shard_map(
        functools.partial(local, mesh.shape["wide"], mesh.shape["narrow"]),
        mesh=mesh,
        in_specs=placed,
        out_specs=P(("wide", "narrow"), None, None),
        check_vma=False,
    )
```

```python
import functools

import jax
import jax.numpy as jnp
from jax import lax
from jax.experimental import pallas as pl
from jax.experimental.pallas import tpu as pltpu
from jax.sharding import PartitionSpec as P

B = 64
K = 7
KC = 7
ROWS = 16
TILES = 32
LANES = 128
HALF = 256
PAIRS = ((1, 2), (3, 4), (5, 6), (0, None))
GROUP = 4
X_CHIPS = 4
F32 = jnp.float32
BF16 = jnp.bfloat16
MESH = pl.DeviceIdType.MESH


def swap(x):
    return pltpu.roll(x, B, 1)


def kernel(
    n_wide,
    n_narrow,
    cols_hbm,
    agg_hbm,
    targ_hbm,
    p_hbm,
    a_hbm,
    out,
    cols,
    agg,
    targ,
    p_raw,
    a_raw,
    p_f32,
    own_pairs,
    sib_pairs,
    far_pairs,
    near_left,
    near_right,
    far_left,
    far_right,
    blocks,
    y_all,
    masked,
    masked_t,
    acc,
    part_out,
    part_in,
    load_sem,
    send_sem,
    recv_sem,
):
    total = n_wide * n_narrow
    me = lax.axis_index("wide") * n_narrow + lax.axis_index("narrow")
    core = me % 2

    def place(index):
        return (index // n_narrow, index % n_narrow)

    def far_of(index):
        return (index - 1 + 2 * (index % 2) + total) % total

    first_wave = me // n_narrow // X_CHIPS < 4
    at_once = jnp.logical_and(first_wave, me % n_narrow // 2 % 2 == 1)
    sibling = place(me + 1 - 2 * core)
    distant = place(far_of(me))

    barrier = pltpu.get_barrier_semaphore()
    for other in (sibling, distant):
        pl.semaphore_signal(barrier, inc=1, device_id=other, device_id_type=MESH)
    operands = ((p_hbm, p_raw), (a_hbm, a_raw), (cols_hbm, cols), (agg_hbm, agg), (targ_hbm, targ))
    loads = [
        pltpu.make_async_copy(source, dest, load_sem.at[n])
        for n, (source, dest) in enumerate(operands)
    ]
    for load in loads:
        load.start()

    def iota(rows, columns):
        shape = (rows, columns)
        return (lax.broadcasted_iota(jnp.int32, shape, 0), lax.broadcasted_iota(jnp.int32, shape, 1))

    def ones_where(condition):
        return jnp.where(condition, 1.0, 0.0).astype(BF16)

    low = iota(ROWS, LANES)[1] < B
    low_block = iota(B, LANES)[1] < B
    low_tiles = iota(TILES, LANES)[1] < B
    low_row = low[:8]

    row, column = iota(HALF, HALF)
    turn = ones_where((row >> 4 == (column & 15)) & ((row & 15) == column >> 4))
    row, column = iota(2 * HALF, HALF)
    turn_twice = ones_where((row >> 5 == (column & 15)) & ((row >> 1 & 15) == column >> 4))

    def stack(tile):
        return jnp.concatenate([tile(t) for t in range(ROWS)], axis=0)

    loads[0].wait()
    flat = jnp.concatenate(
        [
            stack(lambda t, half=half: p_raw[:, pl.ds((half * ROWS + t) * LANES, LANES)])
            for half in range(2)
        ],
        axis=1,
    )
    doubled = jnp.dot(turn_twice, flat, preferred_element_type=F32)
    first_row = (iota(TILES, LANES)[0] & 1) == 0
    for j in range(ROWS // 2):
        for half in range(2):
            lanes = slice(half * LANES, (half + 1) * LANES)
            one = doubled[j * TILES : (j + 1) * TILES, lanes]
            two = doubled[(j + 8) * TILES : (j + 9) * TILES, lanes]
            left = jnp.where(first_row, one, swap(one))
            right = jnp.where(first_row, swap(two), two)
            own_pairs[j, pl.ds(half * TILES, TILES), :] = jnp.where(low_tiles, left, right).astype(BF16)

    to_far = pltpu.make_async_remote_copy(
        own_pairs, far_pairs, send_sem.at[0], recv_sem.at[0], device_id=distant, device_id_type=MESH
    )
    to_sib = pltpu.make_async_remote_copy(
        own_pairs, sib_pairs, send_sem.at[1], recv_sem.at[1], device_id=sibling, device_id_type=MESH
    )

    @pl.when(at_once)
    def _():
        pl.semaphore_wait(barrier, 2)
        to_far.start()
        to_sib.start()

    loads[1].wait()
    for n, (k, other) in enumerate(PAIRS):
        for half in range(2):

            def tile(t, which, half=half):
                return a_raw[which, :, pl.ds((half * ROWS + t) * LANES, LANES)]

            def side(h, t, k=k, other=other, tile=tile):
                one = tile(t, k)[:, h * B : (h + 1) * B]
                two = jnp.zeros_like(one) if other is None else tile(t, other)[:, h * B : (h + 1) * B]
                return jnp.concatenate([one, two], axis=1)

            both = jnp.concatenate(
                [stack(functools.partial(side, h)) for h in range(2)], axis=1
            )
            turned = jnp.dot(turn, both, preferred_element_type=F32).astype(BF16)
            for h in range(2):
                blocks[n, 2 * h + half] = turned[:, h * LANES : (h + 1) * LANES]

    def unpack(source, left, right, start):
        def one(j, carry):
            both = source[j].astype(F32)
            turned = swap(both)
            left[start + j] = jnp.where(low_block, both, 0.0).astype(BF16)
            right[start + j] = jnp.where(low_block, 0.0, turned).astype(BF16)
            left[start + j + 8] = jnp.where(low_block, turned, 0.0).astype(BF16)
            right[start + j + 8] = jnp.where(low_block, 0.0, both).astype(BF16)
            return carry

        lax.fori_loop(0, ROWS // 2, one, 0, unroll=2)

    def clear(left, right, start):
        def one(j, carry):
            left[start + j] = jnp.zeros((B, LANES), BF16)
            right[start + j] = jnp.zeros((B, LANES), BF16)
            return carry

        lax.fori_loop(0, ROWS, one, 0, unroll=4)

    far_start = 2 * ROWS * core
    sib_start = 2 * ROWS - far_start
    clear(near_left, near_right, far_start)
    clear(far_left, far_right, ROWS)
    clear(far_left, far_right, sib_start)
    unpack(own_pairs, near_left, near_right, ROWS)

    for load in loads[2:]:
        load.wait()
    first = me - core
    together = jnp.dot(turn, flat, preferred_element_type=F32)
    p_f32[0] = together[:, :LANES]
    p_f32[1] = together[:, LANES:]

    def mask(i, carry):
        keep = [jnp.where(agg[i] == first + c, 1.0, 0.0) for c in range(2)]
        for half in range(2):
            x = p_f32[half, pl.ds(pl.multiple_of(i * ROWS, ROWS), ROWS), :]
            y = swap(x)
            masked[i, pl.ds(half * ROWS, ROWS), :] = jnp.where(low, x * keep[0], y * keep[1]).astype(BF16)
            masked[i, pl.ds(TILES + half * ROWS, ROWS), :] = jnp.where(
                low, y * keep[0], x * keep[1]
            ).astype(BF16)
        return carry

    lax.fori_loop(0, ROWS, mask, 0, unroll=4)
    row, column = iota(LANES, LANES)
    order = ones_where(column == (row >> 6 << 6) + 2 * (row & 31) + (row >> 5 & 1))
    masked_t[...] = lax.dot_general(
        order,
        masked[...].reshape(ROWS * B, LANES),
        (((1,), (1,)), ((), ())),
        preferred_element_type=F32,
    ).astype(BF16)

    root = (me - 1) * ROWS

    def entry(k, i):
        return jnp.clip(cols[k, i] - root, 0, 3 * ROWS - 1)

    def multiply(pairs, left, right):
        def group(g, carry):
            for r in range(GROUP):
                i = g * GROUP + r
                applied, slots = [], []
                for n, (k, other) in pairs:
                    above = left[entry(k, i)]
                    slot = jnp.full((8, LANES), targ[k, i], jnp.int32)
                    if other is None:
                        below = jnp.zeros((B, LANES), BF16)
                    else:
                        below = right[entry(other, i)]
                        slot = jnp.where(low_row, slot, targ[other, i])
                    rows = pl.ds(pl.multiple_of(i * ROWS, ROWS), ROWS)
                    applied.append(
                        jnp.dot(
                            jnp.concatenate([blocks[n, q, rows, :] for q in range(4)], axis=0),
                            jnp.concatenate([above, below], axis=0),
                            preferred_element_type=F32,
                        )
                    )
                    slots.append(slot)
                for s in range(KC):
                    summed = None
                    for value, slot in zip(applied, slots):
                        keep = jnp.concatenate([jnp.where(slot == s, 1.0, 0.0)] * 8, axis=0)
                        term = value * keep
                        summed = term if summed is None else summed + term
                    y_all[i, :, pl.ds(s * LANES, LANES)] = summed.astype(BF16)
            return carry

        lax.fori_loop(0, ROWS // GROUP, group, 0)
        return jnp.dot(
            masked_t[...],
            y_all[...].reshape(ROWS * B, KC * LANES),
            preferred_element_type=F32,
        )

    numbered = list(enumerate(PAIRS))

    @pl.when(jnp.logical_not(at_once))
    def _():
        pl.semaphore_wait(barrier, 2)
        pl.when(first_wave)(to_far.start)
        to_sib.start()

    to_sib.wait_recv()
    unpack(sib_pairs, near_left, near_right, sib_start)
    acc[...] = multiply(numbered, near_left, near_right)

    pl.when(jnp.logical_not(first_wave))(to_far.start)
    to_far.wait_recv()
    unpack(far_pairs, far_left, far_right, far_start)
    acc[...] += multiply(numbered[:3], far_left, far_right)

    def folded(c, s):
        even = acc[pl.ds(c * B, TILES), pl.ds(s * LANES, LANES)]
        odd = acc[pl.ds(c * B + TILES, TILES), pl.ds(s * LANES, LANES)]
        return jnp.where(low_tiles, even + swap(even), odd + swap(odd))

    for s in range(KC):
        part_out[s] = folded(1 - core, s)
    to_part = pltpu.make_async_remote_copy(
        part_out, part_in, send_sem.at[2], recv_sem.at[2], device_id=sibling, device_id_type=MESH
    )
    to_part.start()
    mine = [folded(core, s) for s in range(KC)]
    to_part.wait_recv()
    for s in range(KC):
        out[s] = mine[s] + part_in[s]
    for copy in (to_far, to_sib, to_part):
        copy.wait_send()


def local(n_wide, n_narrow, a_blocks, p_blocks, columns, aggregate, target):
    hbm = pl.BlockSpec(memory_space=pltpu.HBM)
    vmem = pltpu.VMEM
    smem = pltpu.SMEM
    operands = (columns.T, aggregate, target.T, p_blocks, jnp.transpose(a_blocks, (1, 0, 2)))
    result = pl.pallas_call(
        functools.partial(kernel, n_wide, n_narrow),
        out_shape=jax.ShapeDtypeStruct((KC, TILES, LANES), F32),
        in_specs=[hbm] * 5,
        out_specs=pl.BlockSpec(memory_space=pltpu.VMEM),
        scratch_shapes=[
            smem((K, ROWS), jnp.int32),
            smem((ROWS,), jnp.int32),
            smem((K, ROWS), jnp.int32),
            vmem((ROWS, B * B), BF16),
            vmem((K, ROWS, B * B), BF16),
            vmem((2, HALF, LANES), F32),
            vmem((ROWS // 2, B, LANES), BF16),
            vmem((ROWS // 2, B, LANES), BF16),
            vmem((ROWS // 2, B, LANES), BF16),
            vmem((3 * ROWS, B, LANES), BF16),
            vmem((3 * ROWS, B, LANES), BF16),
            vmem((3 * ROWS, B, LANES), BF16),
            vmem((3 * ROWS, B, LANES), BF16),
            vmem((len(PAIRS), 4, HALF, LANES), BF16),
            vmem((ROWS, B, KC * LANES), BF16),
            vmem((ROWS, B, LANES), BF16),
            vmem((LANES, ROWS * B), BF16),
            vmem((LANES, KC * LANES), F32),
            vmem((KC, TILES, LANES), F32),
            vmem((KC, TILES, LANES), F32),
            pltpu.SemaphoreType.DMA((5,)),
            pltpu.SemaphoreType.DMA((3,)),
            pltpu.SemaphoreType.DMA((3,)),
        ],
        compiler_params=pltpu.CompilerParams(
            collective_id=0, has_side_effects=True, vmem_limit_bytes=40 * 2**20
        ),
    )(*(pltpu.with_memory_space_constraint(value, pltpu.HBM) for value in operands))
    return result.reshape(1, KC, B * B)


def solution(mesh):
    placed = (
        P(("wide", "narrow"), None, None),
        P(("wide", "narrow"), None),
        P(("wide", "narrow"), None),
        P(("wide", "narrow")),
        P(("wide", "narrow"), None),
    )
    return jax.shard_map(
        functools.partial(local, mesh.shape["wide"], mesh.shape["narrow"]),
        mesh=mesh,
        in_specs=placed,
        out_specs=P(("wide", "narrow"), None, None),
        check_vma=False,
    )
```

```python
import functools

import jax
import jax.numpy as jnp
from jax import lax
from jax.experimental import pallas as pl
from jax.experimental.pallas import tpu as pltpu
from jax.sharding import PartitionSpec as P

B = 64
K = 7
KC = 7
ROWS = 16
TILES = 32
LANES = 128
HALF = 256
PAIRS = ((1, 2), (3, 4), (5, 6), (0, None))
GROUP = 4
X_CHIPS = 4
F32 = jnp.float32
BF16 = jnp.bfloat16
MESH = pl.DeviceIdType.MESH


def swap(x):
    return pltpu.roll(x, B, 1)


def kernel(
    n_wide,
    n_narrow,
    cols_hbm,
    agg_hbm,
    targ_hbm,
    p_hbm,
    a_hbm,
    out,
    cols,
    agg,
    targ,
    p_raw,
    a_raw,
    p_f32,
    own_pairs,
    sib_pairs,
    far_pairs,
    passing,
    near_left,
    near_right,
    far_left,
    far_right,
    blocks,
    y_all,
    masked,
    masked_t,
    acc,
    part_out,
    part_in,
    load_sem,
    send_sem,
    recv_sem,
):
    total = n_wide * n_narrow
    me = lax.axis_index("wide") * n_narrow + lax.axis_index("narrow")
    core = me % 2

    def place(index):
        return (index // n_narrow, index % n_narrow)

    def far_of(index):
        return (index - 1 + 2 * (index % 2) + total) % total

    wide, narrow = me // n_narrow, me % n_narrow
    x, z_lo = wide % X_CHIPS, wide // X_CHIPS
    z_run = n_wide // X_CHIPS
    first_wave = jnp.logical_or(z_lo < 4, me == total - 1)
    at_once = jnp.logical_and(first_wave, narrow // 2 % 2 == 1)

    last_x, last = X_CHIPS - 1, n_narrow - 1

    def both(*conditions):
        return functools.reduce(jnp.logical_and, conditions)

    def pick(condition, one, two):
        return tuple(jnp.where(condition, a, b) for a, b in zip(one, two))

    above = both(narrow == last, x == last_x, z_lo < z_run - 1)
    below = both(narrow == 0, x == 0, z_lo > 0)
    relayed = jnp.logical_or(above, below)
    by_above = both(narrow == last - 2, x == last_x, z_lo > 0)
    by_below = both(narrow == 2, x == 0, z_lo < z_run - 1)
    passes = jnp.logical_or(by_above, by_below)
    far = place(far_of(me))
    down = ((z_lo + 1) * X_CHIPS + last_x, last - 2)
    here = (z_lo * X_CHIPS + last_x, last - 2)
    send_to = pick(above, down, pick(below, ((z_lo - 1) * X_CHIPS, 2), far))
    come_from = pick(above, (z_lo * X_CHIPS, 2), pick(below, here, far))
    pass_from = pick(by_above, ((z_lo - 1) * X_CHIPS + last_x, last), ((z_lo + 1) * X_CHIPS, 0))
    pass_to = pick(by_above, (z_lo * X_CHIPS, 0), (z_lo * X_CHIPS + last_x, last))
    sibling = place(me + 1 - 2 * core)

    barrier = pltpu.get_barrier_semaphore()
    for other in (sibling, come_from):
        pl.semaphore_signal(barrier, inc=1, device_id=other, device_id_type=MESH)

    @pl.when(passes)
    def _():
        pl.semaphore_signal(barrier, inc=1, device_id=pass_from, device_id_type=MESH)

    expected = jnp.where(passes, 3, 2)
    operands = ((p_hbm, p_raw), (a_hbm, a_raw), (cols_hbm, cols), (agg_hbm, agg), (targ_hbm, targ))
    loads = [
        pltpu.make_async_copy(source, dest, load_sem.at[n])
        for n, (source, dest) in enumerate(operands)
    ]
    for load in loads:
        load.start()

    def iota(rows, columns):
        shape = (rows, columns)
        return (lax.broadcasted_iota(jnp.int32, shape, 0), lax.broadcasted_iota(jnp.int32, shape, 1))

    def ones_where(condition):
        return jnp.where(condition, 1.0, 0.0).astype(BF16)

    low = iota(ROWS, LANES)[1] < B
    low_block = iota(B, LANES)[1] < B
    low_tiles = iota(TILES, LANES)[1] < B
    low_row = low[:8]

    row, column = iota(HALF, HALF)
    turn = ones_where((row >> 4 == (column & 15)) & ((row & 15) == column >> 4))
    row, column = iota(2 * HALF, HALF)
    turn_twice = ones_where((row >> 5 == (column & 15)) & ((row >> 1 & 15) == column >> 4))

    def stack(tile):
        return jnp.concatenate([tile(t) for t in range(ROWS)], axis=0)

    loads[0].wait()
    flat = jnp.concatenate(
        [
            stack(lambda t, half=half: p_raw[:, pl.ds((half * ROWS + t) * LANES, LANES)])
            for half in range(2)
        ],
        axis=1,
    )
    doubled = jnp.dot(turn_twice, flat, preferred_element_type=F32)
    first_row = (iota(TILES, LANES)[0] & 1) == 0
    for j in range(ROWS // 2):
        for half in range(2):
            lanes = slice(half * LANES, (half + 1) * LANES)
            one = doubled[j * TILES : (j + 1) * TILES, lanes]
            two = doubled[(j + 8) * TILES : (j + 9) * TILES, lanes]
            left = jnp.where(first_row, one, swap(one))
            right = jnp.where(first_row, swap(two), two)
            own_pairs[j, pl.ds(half * TILES, TILES), :] = jnp.where(low_tiles, left, right).astype(BF16)

    def remote(source, dest, n, device):
        return pltpu.make_async_remote_copy(
            source, dest, send_sem.at[n], recv_sem.at[n], device_id=device, device_id_type=MESH
        )

    to_far = remote(own_pairs, far_pairs, 0, send_to)
    to_sib = remote(own_pairs, sib_pairs, 1, sibling)
    to_relay = remote(own_pairs, passing, 3, send_to)
    to_pass = pltpu.make_async_remote_copy(
        passing, far_pairs, send_sem.at[4], recv_sem.at[0], device_id=pass_to, device_id_type=MESH
    )

    def send_far():
        pl.when(jnp.logical_not(relayed))(to_far.start)
        pl.when(relayed)(to_relay.start)

    @pl.when(at_once)
    def _():
        pl.semaphore_wait(barrier, expected)
        send_far()
        to_sib.start()

    loads[1].wait()
    for n, (k, other) in enumerate(PAIRS):
        for half in range(2):

            def tile(t, which, half=half):
                return a_raw[which, :, pl.ds((half * ROWS + t) * LANES, LANES)]

            def side(h, t, k=k, other=other, tile=tile):
                one = tile(t, k)[:, h * B : (h + 1) * B]
                two = jnp.zeros_like(one) if other is None else tile(t, other)[:, h * B : (h + 1) * B]
                return jnp.concatenate([one, two], axis=1)

            both = jnp.concatenate(
                [stack(functools.partial(side, h)) for h in range(2)], axis=1
            )
            turned = jnp.dot(turn, both, preferred_element_type=F32).astype(BF16)
            for h in range(2):
                blocks[n, 2 * h + half] = turned[:, h * LANES : (h + 1) * LANES]

    def unpack(source, left, right, start):
        def one(j, carry):
            both = source[j].astype(F32)
            turned = swap(both)
            left[start + j] = jnp.where(low_block, both, 0.0).astype(BF16)
            right[start + j] = jnp.where(low_block, 0.0, turned).astype(BF16)
            left[start + j + 8] = jnp.where(low_block, turned, 0.0).astype(BF16)
            right[start + j + 8] = jnp.where(low_block, 0.0, both).astype(BF16)
            return carry

        lax.fori_loop(0, ROWS // 2, one, 0, unroll=2)

    def clear(left, right, start):
        def one(j, carry):
            left[start + j] = jnp.zeros((B, LANES), BF16)
            right[start + j] = jnp.zeros((B, LANES), BF16)
            return carry

        lax.fori_loop(0, ROWS, one, 0, unroll=4)

    far_start = 2 * ROWS * core
    sib_start = 2 * ROWS - far_start
    clear(near_left, near_right, far_start)
    clear(far_left, far_right, ROWS)
    clear(far_left, far_right, sib_start)
    unpack(own_pairs, near_left, near_right, ROWS)

    for load in loads[2:]:
        load.wait()
    first = me - core
    together = jnp.dot(turn, flat, preferred_element_type=F32)
    p_f32[0] = together[:, :LANES]
    p_f32[1] = together[:, LANES:]

    def mask(i, carry):
        keep = [jnp.where(agg[i] == first + c, 1.0, 0.0) for c in range(2)]
        for half in range(2):
            x = p_f32[half, pl.ds(pl.multiple_of(i * ROWS, ROWS), ROWS), :]
            y = swap(x)
            masked[i, pl.ds(half * ROWS, ROWS), :] = jnp.where(low, x * keep[0], y * keep[1]).astype(BF16)
            masked[i, pl.ds(TILES + half * ROWS, ROWS), :] = jnp.where(
                low, y * keep[0], x * keep[1]
            ).astype(BF16)
        return carry

    lax.fori_loop(0, ROWS, mask, 0, unroll=4)
    row, column = iota(LANES, LANES)
    order = ones_where(column == (row >> 6 << 6) + 2 * (row & 31) + (row >> 5 & 1))
    masked_t[...] = lax.dot_general(
        order,
        masked[...].reshape(ROWS * B, LANES),
        (((1,), (1,)), ((), ())),
        preferred_element_type=F32,
    ).astype(BF16)

    root = (me - 1) * ROWS

    def entry(k, i):
        return jnp.clip(cols[k, i] - root, 0, 3 * ROWS - 1)

    def multiply(pairs, left, right):
        def group(g, carry):
            for r in range(GROUP):
                i = g * GROUP + r
                applied, slots = [], []
                for n, (k, other) in pairs:
                    above = left[entry(k, i)]
                    slot = jnp.full((8, LANES), targ[k, i], jnp.int32)
                    if other is None:
                        below = jnp.zeros((B, LANES), BF16)
                    else:
                        below = right[entry(other, i)]
                        slot = jnp.where(low_row, slot, targ[other, i])
                    rows = pl.ds(pl.multiple_of(i * ROWS, ROWS), ROWS)
                    applied.append(
                        jnp.dot(
                            jnp.concatenate([blocks[n, q, rows, :] for q in range(4)], axis=0),
                            jnp.concatenate([above, below], axis=0),
                            preferred_element_type=F32,
                        )
                    )
                    slots.append(slot)
                for s in range(KC):
                    summed = None
                    for value, slot in zip(applied, slots):
                        keep = jnp.concatenate([jnp.where(slot == s, 1.0, 0.0)] * 8, axis=0)
                        term = value * keep
                        summed = term if summed is None else summed + term
                    y_all[i, :, pl.ds(s * LANES, LANES)] = summed.astype(BF16)
            return carry

        lax.fori_loop(0, ROWS // GROUP, group, 0)
        return jnp.dot(
            masked_t[...],
            y_all[...].reshape(ROWS * B, KC * LANES),
            preferred_element_type=F32,
        )

    numbered = list(enumerate(PAIRS))

    @pl.when(jnp.logical_not(at_once))
    def _():
        pl.semaphore_wait(barrier, expected)
        pl.when(first_wave)(send_far)
        to_sib.start()

    to_sib.wait_recv()
    unpack(sib_pairs, near_left, near_right, sib_start)
    acc[...] = multiply(numbered, near_left, near_right)

    pl.when(jnp.logical_not(first_wave))(send_far)

    @pl.when(passes)
    def _():
        to_relay.wait_recv()
        to_pass.start()

    to_far.wait_recv()
    unpack(far_pairs, far_left, far_right, far_start)
    acc[...] += multiply(numbered[:3], far_left, far_right)

    def folded(c, s):
        even = acc[pl.ds(c * B, TILES), pl.ds(s * LANES, LANES)]
        odd = acc[pl.ds(c * B + TILES, TILES), pl.ds(s * LANES, LANES)]
        return jnp.where(low_tiles, even + swap(even), odd + swap(odd))

    for s in range(KC):
        part_out[s] = folded(1 - core, s)
    to_part = remote(part_out, part_in, 2, sibling)
    to_part.start()
    mine = [folded(core, s) for s in range(KC)]
    to_part.wait_recv()
    for s in range(KC):
        out[s] = mine[s] + part_in[s]
    pl.when(jnp.logical_not(relayed))(to_far.wait_send)
    pl.when(relayed)(to_relay.wait_send)
    pl.when(passes)(to_pass.wait_send)
    for copy in (to_sib, to_part):
        copy.wait_send()


def local(n_wide, n_narrow, a_blocks, p_blocks, columns, aggregate, target):
    hbm = pl.BlockSpec(memory_space=pltpu.HBM)
    vmem = pltpu.VMEM
    smem = pltpu.SMEM
    operands = (columns.T, aggregate, target.T, p_blocks, jnp.transpose(a_blocks, (1, 0, 2)))
    result = pl.pallas_call(
        functools.partial(kernel, n_wide, n_narrow),
        out_shape=jax.ShapeDtypeStruct((KC, TILES, LANES), F32),
        in_specs=[hbm] * 5,
        out_specs=pl.BlockSpec(memory_space=pltpu.VMEM),
        scratch_shapes=[
            smem((K, ROWS), jnp.int32),
            smem((ROWS,), jnp.int32),
            smem((K, ROWS), jnp.int32),
            vmem((ROWS, B * B), BF16),
            vmem((K, ROWS, B * B), BF16),
            vmem((2, HALF, LANES), F32),
            vmem((ROWS // 2, B, LANES), BF16),
            vmem((ROWS // 2, B, LANES), BF16),
            vmem((ROWS // 2, B, LANES), BF16),
            vmem((ROWS // 2, B, LANES), BF16),
            vmem((3 * ROWS, B, LANES), BF16),
            vmem((3 * ROWS, B, LANES), BF16),
            vmem((3 * ROWS, B, LANES), BF16),
            vmem((3 * ROWS, B, LANES), BF16),
            vmem((len(PAIRS), 4, HALF, LANES), BF16),
            vmem((ROWS, B, KC * LANES), BF16),
            vmem((ROWS, B, LANES), BF16),
            vmem((LANES, ROWS * B), BF16),
            vmem((LANES, KC * LANES), F32),
            vmem((KC, TILES, LANES), F32),
            vmem((KC, TILES, LANES), F32),
            pltpu.SemaphoreType.DMA((5,)),
            pltpu.SemaphoreType.DMA((5,)),
            pltpu.SemaphoreType.DMA((5,)),
        ],
        compiler_params=pltpu.CompilerParams(
            collective_id=0, has_side_effects=True, vmem_limit_bytes=40 * 2**20
        ),
    )(*(pltpu.with_memory_space_constraint(value, pltpu.HBM) for value in operands))
    return result.reshape(1, KC, B * B)


def solution(mesh):
    placed = (
        P(("wide", "narrow"), None, None),
        P(("wide", "narrow"), None),
        P(("wide", "narrow"), None),
        P(("wide", "narrow")),
        P(("wide", "narrow"), None),
    )
    return jax.shard_map(
        functools.partial(local, mesh.shape["wide"], mesh.shape["narrow"]),
        mesh=mesh,
        in_specs=placed,
        out_specs=P(("wide", "narrow"), None, None),
        check_vma=False,
    )
```

```python
import functools

import jax
import jax.numpy as jnp
from jax import lax
from jax.experimental import pallas as pl
from jax.experimental.pallas import tpu as pltpu
from jax.sharding import PartitionSpec as P

B = 64
K = 7
KC = 7
ROWS = 16
TILES = 32
LANES = 128
HALF = 256
PAIRS = ((1, 2), (3, 4), (5, 6), (0, None))
GROUP = 4
X_CHIPS = 4
CHUNKS = 4
F32 = jnp.float32
BF16 = jnp.bfloat16
MESH = pl.DeviceIdType.MESH


def swap(x):
    return pltpu.roll(x, B, 1)


def kernel(
    n_wide,
    n_narrow,
    cols_hbm,
    agg_hbm,
    targ_hbm,
    p_hbm,
    a_hbm,
    out,
    cols,
    agg,
    targ,
    p_raw,
    a_raw,
    p_f32,
    own_pairs,
    sib_pairs,
    far_pairs,
    passing,
    near_left,
    near_right,
    far_left,
    far_right,
    blocks,
    y_all,
    masked,
    masked_t,
    acc,
    part_out,
    part_in,
    load_sem,
    send_sem,
    recv_sem,
):
    total = n_wide * n_narrow
    me = lax.axis_index("wide") * n_narrow + lax.axis_index("narrow")
    core = me % 2

    def place(index):
        return (index // n_narrow, index % n_narrow)

    def far_of(index):
        return (index - 1 + 2 * (index % 2) + total) % total

    def relay_of(index, flipped):
        wide, narrow = index // n_narrow, index % n_narrow
        z_lo, x = wide // X_CHIPS, wide % X_CHIPS
        flip = (z_lo + index % 2 + flipped) % 2
        z_hi = narrow // 2 % 2
        wide = (z_lo + 1 - 2 * (z_lo % 2)) * X_CHIPS + x
        return wide * n_narrow + narrow + flip * (2 - 4 * z_hi)

    def in_first(index):
        return jnp.logical_or(index // n_narrow // X_CHIPS < 4, index == total - 1)

    source = relay_of(me, 1)
    first_wave = in_first(me)
    at_once = jnp.logical_and(first_wave, me % n_narrow // 2 % 2 == 1)
    quick = jnp.logical_and((me // n_narrow // X_CHIPS + core) % 2 == 1, in_first(source))
    sibling = place(me + 1 - 2 * core)
    relay = place(relay_of(me, 0))
    onward = place(far_of(source))

    barrier = pltpu.get_barrier_semaphore()
    for other in (sibling, place(source), place(relay_of(far_of(me), 0))):
        pl.semaphore_signal(barrier, inc=1, device_id=other, device_id_type=MESH)
    operands = ((p_hbm, p_raw), (a_hbm, a_raw), (cols_hbm, cols), (agg_hbm, agg), (targ_hbm, targ))
    loads = [
        pltpu.make_async_copy(source, dest, load_sem.at[n])
        for n, (source, dest) in enumerate(operands)
    ]
    for load in loads:
        load.start()

    def iota(rows, columns):
        shape = (rows, columns)
        return (lax.broadcasted_iota(jnp.int32, shape, 0), lax.broadcasted_iota(jnp.int32, shape, 1))

    def ones_where(condition):
        return jnp.where(condition, 1.0, 0.0).astype(BF16)

    low = iota(ROWS, LANES)[1] < B
    low_block = iota(B, LANES)[1] < B
    low_tiles = iota(TILES, LANES)[1] < B
    low_row = low[:8]

    row, column = iota(HALF, HALF)
    turn = ones_where((row >> 4 == (column & 15)) & ((row & 15) == column >> 4))
    row, column = iota(2 * HALF, HALF)
    turn_twice = ones_where((row >> 5 == (column & 15)) & ((row >> 1 & 15) == column >> 4))

    def stack(tile):
        return jnp.concatenate([tile(t) for t in range(ROWS)], axis=0)

    loads[0].wait()
    flat = jnp.concatenate(
        [
            stack(lambda t, half=half: p_raw[:, pl.ds((half * ROWS + t) * LANES, LANES)])
            for half in range(2)
        ],
        axis=1,
    )
    doubled = jnp.dot(turn_twice, flat, preferred_element_type=F32)
    first_row = (iota(TILES, LANES)[0] & 1) == 0
    for j in range(ROWS // 2):
        for half in range(2):
            lanes = slice(half * LANES, (half + 1) * LANES)
            one = doubled[j * TILES : (j + 1) * TILES, lanes]
            two = doubled[(j + 8) * TILES : (j + 9) * TILES, lanes]
            left = jnp.where(first_row, one, swap(one))
            right = jnp.where(first_row, swap(two), two)
            own_pairs[j, pl.ds(half * TILES, TILES), :] = jnp.where(low_tiles, left, right).astype(BF16)

    def remote(source, dest, n, device):
        return pltpu.make_async_remote_copy(
            source, dest, send_sem.at[n], recv_sem.at[n], device_id=device, device_id_type=MESH
        )

    chunks = [pl.ds(n * 2, 2) for n in range(CHUNKS)]
    to_sib = remote(own_pairs, sib_pairs, 0, sibling)
    to_relay = [
        remote(own_pairs.at[chunk], passing.at[chunk], 2 + n, relay) for n, chunk in enumerate(chunks)
    ]
    to_onward = [
        remote(passing.at[chunk], far_pairs.at[chunk], 2 + CHUNKS + n, onward)
        for n, chunk in enumerate(chunks)
    ]

    def send_far():
        for copy in to_relay:
            copy.start()

    def pass_on(n):
        to_relay[n].wait_recv()
        to_onward[n].start()

    def pass_all():
        for n in range(CHUNKS):
            pass_on(n)

    pass_between = jnp.logical_and(at_once, quick)
    pass_after = jnp.logical_and(jnp.logical_not(at_once), quick)
    pass_half_way = jnp.logical_and(at_once, jnp.logical_not(quick))
    pass_last = jnp.logical_not(jnp.logical_or(at_once, quick))

    @pl.when(at_once)
    def _():
        pl.semaphore_wait(barrier, 3)
        send_far()
        to_sib.start()

    loads[1].wait()
    for n, (k, other) in enumerate(PAIRS):
        for half in range(2):

            def tile(t, which, half=half):
                return a_raw[which, :, pl.ds((half * ROWS + t) * LANES, LANES)]

            def side(h, t, k=k, other=other, tile=tile):
                one = tile(t, k)[:, h * B : (h + 1) * B]
                two = jnp.zeros_like(one) if other is None else tile(t, other)[:, h * B : (h + 1) * B]
                return jnp.concatenate([one, two], axis=1)

            both = jnp.concatenate(
                [stack(functools.partial(side, h)) for h in range(2)], axis=1
            )
            turned = jnp.dot(turn, both, preferred_element_type=F32).astype(BF16)
            for h in range(2):
                blocks[n, 2 * h + half] = turned[:, h * LANES : (h + 1) * LANES]
        pl.when(pass_between)(functools.partial(pass_on, n))

    def unpack(source, left, right, start, begin=0, end=ROWS // 2):
        def one(j, carry):
            both = source[j].astype(F32)
            turned = swap(both)
            left[start + j] = jnp.where(low_block, both, 0.0).astype(BF16)
            right[start + j] = jnp.where(low_block, 0.0, turned).astype(BF16)
            left[start + j + 8] = jnp.where(low_block, turned, 0.0).astype(BF16)
            right[start + j + 8] = jnp.where(low_block, 0.0, both).astype(BF16)
            return carry

        lax.fori_loop(begin, end, one, 0, unroll=2)

    def clear(left, right, start):
        def one(j, carry):
            left[start + j] = jnp.zeros((B, LANES), BF16)
            right[start + j] = jnp.zeros((B, LANES), BF16)
            return carry

        lax.fori_loop(0, ROWS, one, 0, unroll=4)

    far_start = 2 * ROWS * core
    sib_start = 2 * ROWS - far_start
    clear(near_left, near_right, far_start)
    clear(far_left, far_right, ROWS)
    clear(far_left, far_right, sib_start)
    unpack(own_pairs, near_left, near_right, ROWS)

    for load in loads[2:]:
        load.wait()
    first = me - core
    together = jnp.dot(turn, flat, preferred_element_type=F32)
    p_f32[0] = together[:, :LANES]
    p_f32[1] = together[:, LANES:]

    def mask(i, carry):
        keep = [jnp.where(agg[i] == first + c, 1.0, 0.0) for c in range(2)]
        for half in range(2):
            x = p_f32[half, pl.ds(pl.multiple_of(i * ROWS, ROWS), ROWS), :]
            y = swap(x)
            masked[i, pl.ds(half * ROWS, ROWS), :] = jnp.where(low, x * keep[0], y * keep[1]).astype(BF16)
            masked[i, pl.ds(TILES + half * ROWS, ROWS), :] = jnp.where(
                low, y * keep[0], x * keep[1]
            ).astype(BF16)
        return carry

    lax.fori_loop(0, ROWS, mask, 0, unroll=4)
    row, column = iota(LANES, LANES)
    order = ones_where(column == (row >> 6 << 6) + 2 * (row & 31) + (row >> 5 & 1))
    masked_t[...] = lax.dot_general(
        order,
        masked[...].reshape(ROWS * B, LANES),
        (((1,), (1,)), ((), ())),
        preferred_element_type=F32,
    ).astype(BF16)

    root = (me - 1) * ROWS

    def entry(k, i):
        return jnp.clip(cols[k, i] - root, 0, 3 * ROWS - 1)

    def multiply(pairs, left, right, half_way):
        def group(g, carry):
            for r in range(GROUP):
                i = g * GROUP + r
                applied, slots = [], []
                for n, (k, other) in pairs:
                    above = left[entry(k, i)]
                    slot = jnp.full((8, LANES), targ[k, i], jnp.int32)
                    if other is None:
                        below = jnp.zeros((B, LANES), BF16)
                    else:
                        below = right[entry(other, i)]
                        slot = jnp.where(low_row, slot, targ[other, i])
                    rows = pl.ds(pl.multiple_of(i * ROWS, ROWS), ROWS)
                    applied.append(
                        jnp.dot(
                            jnp.concatenate([blocks[n, q, rows, :] for q in range(4)], axis=0),
                            jnp.concatenate([above, below], axis=0),
                            preferred_element_type=F32,
                        )
                    )
                    slots.append(slot)
                for s in range(KC):
                    summed = None
                    for value, slot in zip(applied, slots):
                        keep = jnp.concatenate([jnp.where(slot == s, 1.0, 0.0)] * 8, axis=0)
                        term = value * keep
                        summed = term if summed is None else summed + term
                    y_all[i, :, pl.ds(s * LANES, LANES)] = summed.astype(BF16)
            return carry

        lax.fori_loop(0, 2, group, 0)
        half_way()
        lax.fori_loop(2, 4, group, 0)
        return jnp.dot(
            masked_t[...],
            y_all[...].reshape(ROWS * B, KC * LANES),
            preferred_element_type=F32,
        )

    numbered = list(enumerate(PAIRS))

    @pl.when(jnp.logical_not(at_once))
    def _():
        pl.semaphore_wait(barrier, 3)
        pl.when(first_wave)(send_far)
        to_sib.start()

    pl.when(pass_after)(pass_all)
    to_sib.wait_recv()
    unpack(sib_pairs, near_left, near_right, sib_start)

    def half_way():
        pl.when(jnp.logical_not(first_wave))(send_far)
        pl.when(pass_half_way)(pass_all)

    acc[...] = multiply(numbered, near_left, near_right, half_way)

    pl.when(pass_last)(pass_all)
    for n, copy in enumerate(to_onward):
        copy.wait_recv()
        unpack(far_pairs, far_left, far_right, far_start, 2 * n, 2 * n + 2)
    acc[...] += multiply(numbered[:3], far_left, far_right, lambda: None)

    def folded(c, s):
        even = acc[pl.ds(c * B, TILES), pl.ds(s * LANES, LANES)]
        odd = acc[pl.ds(c * B + TILES, TILES), pl.ds(s * LANES, LANES)]
        return jnp.where(low_tiles, even + swap(even), odd + swap(odd))

    for s in range(KC):
        part_out[s] = folded(1 - core, s)
    to_part = remote(part_out, part_in, 1, sibling)
    to_part.start()
    mine = [folded(core, s) for s in range(KC)]
    to_part.wait_recv()
    for s in range(KC):
        out[s] = mine[s] + part_in[s]
    for copy in (*to_relay, *to_onward, to_sib, to_part):
        copy.wait_send()


def local(n_wide, n_narrow, a_blocks, p_blocks, columns, aggregate, target):
    hbm = pl.BlockSpec(memory_space=pltpu.HBM)
    vmem = pltpu.VMEM
    smem = pltpu.SMEM
    operands = (columns.T, aggregate, target.T, p_blocks, jnp.transpose(a_blocks, (1, 0, 2)))
    result = pl.pallas_call(
        functools.partial(kernel, n_wide, n_narrow),
        out_shape=jax.ShapeDtypeStruct((KC, TILES, LANES), F32),
        in_specs=[hbm] * 5,
        out_specs=pl.BlockSpec(memory_space=pltpu.VMEM),
        scratch_shapes=[
            smem((K, ROWS), jnp.int32),
            smem((ROWS,), jnp.int32),
            smem((K, ROWS), jnp.int32),
            vmem((ROWS, B * B), BF16),
            vmem((K, ROWS, B * B), BF16),
            vmem((2, HALF, LANES), F32),
            vmem((ROWS // 2, B, LANES), BF16),
            vmem((ROWS // 2, B, LANES), BF16),
            vmem((ROWS // 2, B, LANES), BF16),
            vmem((ROWS // 2, B, LANES), BF16),
            vmem((3 * ROWS, B, LANES), BF16),
            vmem((3 * ROWS, B, LANES), BF16),
            vmem((3 * ROWS, B, LANES), BF16),
            vmem((3 * ROWS, B, LANES), BF16),
            vmem((len(PAIRS), 4, HALF, LANES), BF16),
            vmem((ROWS, B, KC * LANES), BF16),
            vmem((ROWS, B, LANES), BF16),
            vmem((LANES, ROWS * B), BF16),
            vmem((LANES, KC * LANES), F32),
            vmem((KC, TILES, LANES), F32),
            vmem((KC, TILES, LANES), F32),
            pltpu.SemaphoreType.DMA((5,)),
            pltpu.SemaphoreType.DMA((2 + 2 * CHUNKS,)),
            pltpu.SemaphoreType.DMA((2 + 2 * CHUNKS,)),
        ],
        compiler_params=pltpu.CompilerParams(
            collective_id=0, has_side_effects=True, vmem_limit_bytes=40 * 2**20
        ),
    )(*(pltpu.with_memory_space_constraint(value, pltpu.HBM) for value in operands))
    return result.reshape(1, KC, B * B)


def solution(mesh):
    placed = (
        P(("wide", "narrow"), None, None),
        P(("wide", "narrow"), None),
        P(("wide", "narrow"), None),
        P(("wide", "narrow")),
        P(("wide", "narrow"), None),
    )
    return jax.shard_map(
        functools.partial(local, mesh.shape["wide"], mesh.shape["narrow"]),
        mesh=mesh,
        in_specs=placed,
        out_specs=P(("wide", "narrow"), None, None),
        check_vma=False,
    )
```

```python
import functools

import jax
import jax.numpy as jnp
from jax import lax
from jax.experimental import pallas as pl
from jax.experimental.pallas import tpu as pltpu
from jax.sharding import PartitionSpec as P

B = 64
K = 7
KC = 7
ROWS = 16
TILES = 32
LANES = 128
HALF = 256
PAIRS = ((1, 2), (3, 4), (5, 6), (0, None))
GROUP = 4
X_CHIPS = 4
F32 = jnp.float32
BF16 = jnp.bfloat16
MESH = pl.DeviceIdType.MESH


def swap(x):
    return pltpu.roll(x, B, 1)


def kernel(
    n_wide,
    n_narrow,
    cols_hbm,
    agg_hbm,
    targ_hbm,
    p_hbm,
    a_hbm,
    out,
    cols,
    agg,
    targ,
    p_raw,
    a_raw,
    p_f32,
    own_pairs,
    sib_pairs,
    far_pairs,
    passing,
    near_left,
    near_right,
    far_left,
    far_right,
    blocks,
    y_all,
    masked,
    masked_t,
    acc,
    part_out,
    part_in,
    load_sem,
    send_sem,
    recv_sem,
):
    total = n_wide * n_narrow
    me = lax.axis_index("wide") * n_narrow + lax.axis_index("narrow")
    core = me % 2

    def place(index):
        return (index // n_narrow, index % n_narrow)

    def far_of(index):
        return (index - 1 + 2 * (index % 2) + total) % total

    wide, narrow = me // n_narrow, me % n_narrow
    x, z_lo = wide % X_CHIPS, wide // X_CHIPS
    z_run = n_wide // X_CHIPS
    last_x, last = X_CHIPS - 1, n_narrow - 1

    def both(*conditions):
        return functools.reduce(jnp.logical_and, conditions)

    def pick(condition, one, two):
        return tuple(jnp.where(condition, a, b) for a, b in zip(one, two))

    first_wave = jnp.logical_or(z_lo < 4, me == total - 1)
    at_once = jnp.logical_and(first_wave, narrow // 2 % 2 == 1)

    odd = z_lo % 2 == 1
    above = both(narrow == last, x == last_x, z_lo < z_run - 1, odd)
    below = both(narrow == 0, x == 0, z_lo > 0, jnp.logical_not(odd))
    relayed = jnp.logical_or(above, below)
    by_above = both(narrow == last - 1, x == last_x, z_lo > 2, odd)
    by_below = both(narrow == 1, x == 0, z_lo < z_run - 3, jnp.logical_not(odd))
    passes = jnp.logical_or(by_above, by_below)
    far = place(far_of(me))
    on_above = ((z_lo + 2) * X_CHIPS + last_x, last - 1)
    on_below = ((z_lo - 2) * X_CHIPS, 1)
    send_to = pick(above, on_above, pick(below, on_below, far))
    come_from = pick(above, ((z_lo - 1) * X_CHIPS, 1), pick(below, ((z_lo + 1) * X_CHIPS + last_x, last - 1), far))
    pass_from = pick(by_above, ((z_lo - 2) * X_CHIPS + last_x, last), ((z_lo + 2) * X_CHIPS, 0))
    pass_to = pick(by_above, ((z_lo - 1) * X_CHIPS, 0), ((z_lo + 1) * X_CHIPS + last_x, last))
    sibling = place(me + 1 - 2 * core)

    barrier = pltpu.get_barrier_semaphore()

    def greet(other):
        pl.semaphore_signal(barrier, inc=1, device_id=other, device_id_type=MESH)

    greet(sibling)
    greet(come_from)
    pl.when(passes)(functools.partial(greet, pass_from))
    expected = 2 + jnp.where(passes, 1, 0)
    operands = ((p_hbm, p_raw), (a_hbm, a_raw), (cols_hbm, cols), (agg_hbm, agg), (targ_hbm, targ))
    loads = [
        pltpu.make_async_copy(source, dest, load_sem.at[n])
        for n, (source, dest) in enumerate(operands)
    ]
    for load in loads:
        load.start()

    def iota(rows, columns):
        shape = (rows, columns)
        return (lax.broadcasted_iota(jnp.int32, shape, 0), lax.broadcasted_iota(jnp.int32, shape, 1))

    def ones_where(condition):
        return jnp.where(condition, 1.0, 0.0).astype(BF16)

    low = iota(ROWS, LANES)[1] < B
    low_block = iota(B, LANES)[1] < B
    low_tiles = iota(TILES, LANES)[1] < B
    low_row = low[:8]

    row, column = iota(HALF, HALF)
    turn = ones_where((row >> 4 == (column & 15)) & ((row & 15) == column >> 4))
    row, column = iota(2 * HALF, HALF)
    turn_twice = ones_where((row >> 5 == (column & 15)) & ((row >> 1 & 15) == column >> 4))

    def stack(tile):
        return jnp.concatenate([tile(t) for t in range(ROWS)], axis=0)

    loads[0].wait()
    flat = jnp.concatenate(
        [
            stack(lambda t, half=half: p_raw[:, pl.ds((half * ROWS + t) * LANES, LANES)])
            for half in range(2)
        ],
        axis=1,
    )
    doubled = jnp.dot(turn_twice, flat, preferred_element_type=F32)
    first_row = (iota(TILES, LANES)[0] & 1) == 0
    for j in range(ROWS // 2):
        for half in range(2):
            lanes = slice(half * LANES, (half + 1) * LANES)
            one = doubled[j * TILES : (j + 1) * TILES, lanes]
            two = doubled[(j + 8) * TILES : (j + 9) * TILES, lanes]
            left = jnp.where(first_row, one, swap(one))
            right = jnp.where(first_row, swap(two), two)
            own_pairs[j, pl.ds(half * TILES, TILES), :] = jnp.where(low_tiles, left, right).astype(BF16)

    def remote(source, dest, n, device):
        return pltpu.make_async_remote_copy(
            source, dest, send_sem.at[n], recv_sem.at[n], device_id=device, device_id_type=MESH
        )

    to_far = remote(own_pairs, far_pairs, 0, send_to)
    to_sib = remote(own_pairs, sib_pairs, 1, sibling)
    to_relay = remote(own_pairs, passing, 3, send_to)
    to_pass = pltpu.make_async_remote_copy(
        passing, far_pairs, send_sem.at[4], recv_sem.at[0], device_id=pass_to, device_id_type=MESH
    )

    def send_far():
        pl.when(jnp.logical_not(relayed))(to_far.start)
        pl.when(relayed)(to_relay.start)

    @pl.when(at_once)
    def _():
        pl.semaphore_wait(barrier, expected)
        send_far()
        to_sib.start()

    loads[1].wait()
    for n, (k, other) in enumerate(PAIRS):
        for half in range(2):

            def tile(t, which, half=half):
                return a_raw[which, :, pl.ds((half * ROWS + t) * LANES, LANES)]

            def side(h, t, k=k, other=other, tile=tile):
                one = tile(t, k)[:, h * B : (h + 1) * B]
                two = jnp.zeros_like(one) if other is None else tile(t, other)[:, h * B : (h + 1) * B]
                return jnp.concatenate([one, two], axis=1)

            both = jnp.concatenate(
                [stack(functools.partial(side, h)) for h in range(2)], axis=1
            )
            turned = jnp.dot(turn, both, preferred_element_type=F32).astype(BF16)
            for h in range(2):
                blocks[n, 2 * h + half] = turned[:, h * LANES : (h + 1) * LANES]

    def unpack(source, left, right, start):
        def one(j, carry):
            both = source[j].astype(F32)
            turned = swap(both)
            left[start + j] = jnp.where(low_block, both, 0.0).astype(BF16)
            right[start + j] = jnp.where(low_block, 0.0, turned).astype(BF16)
            left[start + j + 8] = jnp.where(low_block, turned, 0.0).astype(BF16)
            right[start + j + 8] = jnp.where(low_block, 0.0, both).astype(BF16)
            return carry

        lax.fori_loop(0, ROWS // 2, one, 0, unroll=2)

    def clear(left, right, start):
        def one(j, carry):
            left[start + j] = jnp.zeros((B, LANES), BF16)
            right[start + j] = jnp.zeros((B, LANES), BF16)
            return carry

        lax.fori_loop(0, ROWS, one, 0, unroll=4)

    far_start = 2 * ROWS * core
    sib_start = 2 * ROWS - far_start
    clear(near_left, near_right, far_start)
    clear(far_left, far_right, ROWS)
    clear(far_left, far_right, sib_start)
    unpack(own_pairs, near_left, near_right, ROWS)

    for load in loads[2:]:
        load.wait()
    first = me - core
    together = jnp.dot(turn, flat, preferred_element_type=F32)
    p_f32[0] = together[:, :LANES]
    p_f32[1] = together[:, LANES:]

    def mask(i, carry):
        keep = [jnp.where(agg[i] == first + c, 1.0, 0.0) for c in range(2)]
        for half in range(2):
            x = p_f32[half, pl.ds(pl.multiple_of(i * ROWS, ROWS), ROWS), :]
            y = swap(x)
            masked[i, pl.ds(half * ROWS, ROWS), :] = jnp.where(low, x * keep[0], y * keep[1]).astype(BF16)
            masked[i, pl.ds(TILES + half * ROWS, ROWS), :] = jnp.where(
                low, y * keep[0], x * keep[1]
            ).astype(BF16)
        return carry

    lax.fori_loop(0, ROWS, mask, 0, unroll=4)
    row, column = iota(LANES, LANES)
    order = ones_where(column == (row >> 6 << 6) + 2 * (row & 31) + (row >> 5 & 1))
    masked_t[...] = lax.dot_general(
        order,
        masked[...].reshape(ROWS * B, LANES),
        (((1,), (1,)), ((), ())),
        preferred_element_type=F32,
    ).astype(BF16)

    root = (me - 1) * ROWS

    def entry(k, i):
        return jnp.clip(cols[k, i] - root, 0, 3 * ROWS - 1)

    def multiply(pairs, left, right):
        def group(g, carry):
            for r in range(GROUP):
                i = g * GROUP + r
                applied, slots = [], []
                for n, (k, other) in pairs:
                    above = left[entry(k, i)]
                    slot = jnp.full((8, LANES), targ[k, i], jnp.int32)
                    if other is None:
                        below = jnp.zeros((B, LANES), BF16)
                    else:
                        below = right[entry(other, i)]
                        slot = jnp.where(low_row, slot, targ[other, i])
                    rows = pl.ds(pl.multiple_of(i * ROWS, ROWS), ROWS)
                    applied.append(
                        jnp.dot(
                            jnp.concatenate([blocks[n, q, rows, :] for q in range(4)], axis=0),
                            jnp.concatenate([above, below], axis=0),
                            preferred_element_type=F32,
                        )
                    )
                    slots.append(slot)
                for s in range(KC):
                    summed = None
                    for value, slot in zip(applied, slots):
                        keep = jnp.concatenate([jnp.where(slot == s, 1.0, 0.0)] * 8, axis=0)
                        term = value * keep
                        summed = term if summed is None else summed + term
                    y_all[i, :, pl.ds(s * LANES, LANES)] = summed.astype(BF16)
            return carry

        lax.fori_loop(0, ROWS // GROUP, group, 0)
        return jnp.dot(
            masked_t[...],
            y_all[...].reshape(ROWS * B, KC * LANES),
            preferred_element_type=F32,
        )

    numbered = list(enumerate(PAIRS))

    @pl.when(jnp.logical_not(at_once))
    def _():
        pl.semaphore_wait(barrier, expected)
        pl.when(first_wave)(send_far)
        to_sib.start()

    to_sib.wait_recv()
    unpack(sib_pairs, near_left, near_right, sib_start)
    acc[...] = multiply(numbered, near_left, near_right)

    pl.when(jnp.logical_not(first_wave))(send_far)

    @pl.when(passes)
    def _():
        to_relay.wait_recv()
        to_pass.start()

    to_far.wait_recv()
    unpack(far_pairs, far_left, far_right, far_start)
    acc[...] += multiply(numbered[:3], far_left, far_right)

    def folded(c, s):
        even = acc[pl.ds(c * B, TILES), pl.ds(s * LANES, LANES)]
        odd = acc[pl.ds(c * B + TILES, TILES), pl.ds(s * LANES, LANES)]
        return jnp.where(low_tiles, even + swap(even), odd + swap(odd))

    for s in range(KC):
        part_out[s] = folded(1 - core, s)
    to_part = remote(part_out, part_in, 2, sibling)
    to_part.start()
    mine = [folded(core, s) for s in range(KC)]
    to_part.wait_recv()
    for s in range(KC):
        out[s] = mine[s] + part_in[s]
    pl.when(jnp.logical_not(relayed))(to_far.wait_send)
    pl.when(relayed)(to_relay.wait_send)
    pl.when(passes)(to_pass.wait_send)
    for copy in (to_sib, to_part):
        copy.wait_send()


def local(n_wide, n_narrow, a_blocks, p_blocks, columns, aggregate, target):
    hbm = pl.BlockSpec(memory_space=pltpu.HBM)
    vmem = pltpu.VMEM
    smem = pltpu.SMEM
    operands = (columns.T, aggregate, target.T, p_blocks, jnp.transpose(a_blocks, (1, 0, 2)))
    result = pl.pallas_call(
        functools.partial(kernel, n_wide, n_narrow),
        out_shape=jax.ShapeDtypeStruct((KC, TILES, LANES), F32),
        in_specs=[hbm] * 5,
        out_specs=pl.BlockSpec(memory_space=pltpu.VMEM),
        scratch_shapes=[
            smem((K, ROWS), jnp.int32),
            smem((ROWS,), jnp.int32),
            smem((K, ROWS), jnp.int32),
            vmem((ROWS, B * B), BF16),
            vmem((K, ROWS, B * B), BF16),
            vmem((2, HALF, LANES), F32),
            vmem((ROWS // 2, B, LANES), BF16),
            vmem((ROWS // 2, B, LANES), BF16),
            vmem((ROWS // 2, B, LANES), BF16),
            vmem((ROWS // 2, B, LANES), BF16),
            vmem((3 * ROWS, B, LANES), BF16),
            vmem((3 * ROWS, B, LANES), BF16),
            vmem((3 * ROWS, B, LANES), BF16),
            vmem((3 * ROWS, B, LANES), BF16),
            vmem((len(PAIRS), 4, HALF, LANES), BF16),
            vmem((ROWS, B, KC * LANES), BF16),
            vmem((ROWS, B, LANES), BF16),
            vmem((LANES, ROWS * B), BF16),
            vmem((LANES, KC * LANES), F32),
            vmem((KC, TILES, LANES), F32),
            vmem((KC, TILES, LANES), F32),
            pltpu.SemaphoreType.DMA((5,)),
            pltpu.SemaphoreType.DMA((5,)),
            pltpu.SemaphoreType.DMA((5,)),
        ],
        compiler_params=pltpu.CompilerParams(
            collective_id=0, has_side_effects=True, vmem_limit_bytes=40 * 2**20
        ),
    )(*(pltpu.with_memory_space_constraint(value, pltpu.HBM) for value in operands))
    return result.reshape(1, KC, B * B)


def solution(mesh):
    placed = (
        P(("wide", "narrow"), None, None),
        P(("wide", "narrow"), None),
        P(("wide", "narrow"), None),
        P(("wide", "narrow")),
        P(("wide", "narrow"), None),
    )
    return jax.shard_map(
        functools.partial(local, mesh.shape["wide"], mesh.shape["narrow"]),
        mesh=mesh,
        in_specs=placed,
        out_specs=P(("wide", "narrow"), None, None),
        check_vma=False,
    )
```

```python
import functools

import jax
import jax.numpy as jnp
from jax import lax
from jax.experimental import pallas as pl
from jax.experimental.pallas import tpu as pltpu
from jax.sharding import PartitionSpec as P

B = 64
K = 7
KC = 7
ROWS = 16
TILES = 32
LANES = 128
HALF = 256
PAIRS = ((1, 2), (3, 4), (5, 6), (0, None))
GROUP = 4
X_CHIPS = 4
F32 = jnp.float32
BF16 = jnp.bfloat16
MESH = pl.DeviceIdType.MESH


def swap(x):
    return pltpu.roll(x, B, 1)


def kernel(
    n_wide,
    n_narrow,
    cols_hbm,
    agg_hbm,
    targ_hbm,
    p_hbm,
    a_hbm,
    out,
    cols,
    agg,
    targ,
    p_raw,
    a_raw,
    p_f32,
    own_pairs,
    sib_pairs,
    far_pairs,
    passing,
    near_left,
    near_right,
    far_left,
    far_right,
    blocks,
    y_all,
    masked,
    masked_t,
    acc,
    part_out,
    part_in,
    load_sem,
    send_sem,
    recv_sem,
    go_sem,
):
    total = n_wide * n_narrow
    me = lax.axis_index("wide") * n_narrow + lax.axis_index("narrow")
    core = me % 2

    def place(index):
        return (index // n_narrow, index % n_narrow)

    def far_of(index):
        return (index - 1 + 2 * (index % 2) + total) % total

    wide, narrow = me // n_narrow, me % n_narrow
    x, z_lo = wide % X_CHIPS, wide // X_CHIPS
    z_run = n_wide // X_CHIPS
    last_x, last = X_CHIPS - 1, n_narrow - 1

    def both(*conditions):
        return functools.reduce(jnp.logical_and, conditions)

    def pick(condition, one, two):
        return tuple(jnp.where(condition, a, b) for a, b in zip(one, two))

    quarter = z_run // 4
    step = quarter * X_CHIPS * n_narrow
    first_wave = jnp.logical_or(z_lo < 2 * quarter, me == total - 1)
    at_once = jnp.logical_and(first_wave, narrow // 2 % 2 == 1)
    second_wave = jnp.logical_and(z_lo >= 2 * quarter, z_lo < 3 * quarter)
    third_wave = jnp.logical_and(z_lo >= 3 * quarter, me != total - 1)
    lets = jnp.logical_and(second_wave, me + step != total - 1)
    held_up = place((me - step + total) % total)
    let_go = place((me + step) % total)

    odd = z_lo % 2 == 1
    above = both(narrow == last, x == last_x, z_lo < z_run - 1, odd)
    below = both(narrow == 0, x == 0, z_lo > 0, jnp.logical_not(odd))
    relayed = jnp.logical_or(above, below)
    by_above = both(narrow == last - 1, x == last_x, z_lo > 2, odd)
    by_below = both(narrow == 1, x == 0, z_lo < z_run - 3, jnp.logical_not(odd))
    passes = jnp.logical_or(by_above, by_below)
    far = place(far_of(me))
    on_above = ((z_lo + 2) * X_CHIPS + last_x, last - 1)
    on_below = ((z_lo - 2) * X_CHIPS, 1)
    send_to = pick(above, on_above, pick(below, on_below, far))
    come_from = pick(above, ((z_lo - 1) * X_CHIPS, 1), pick(below, ((z_lo + 1) * X_CHIPS + last_x, last - 1), far))
    pass_from = pick(by_above, ((z_lo - 2) * X_CHIPS + last_x, last), ((z_lo + 2) * X_CHIPS, 0))
    pass_to = pick(by_above, ((z_lo - 1) * X_CHIPS, 0), ((z_lo + 1) * X_CHIPS + last_x, last))
    sibling = place(me + 1 - 2 * core)

    barrier = pltpu.get_barrier_semaphore()

    def greet(other):
        pl.semaphore_signal(barrier, inc=1, device_id=other, device_id_type=MESH)

    greet(sibling)
    greet(come_from)
    pl.when(passes)(functools.partial(greet, pass_from))
    pl.when(third_wave)(functools.partial(greet, held_up))
    expected = 2 + jnp.where(passes, 1, 0) + jnp.where(lets, 1, 0)
    operands = ((p_hbm, p_raw), (a_hbm, a_raw), (cols_hbm, cols), (agg_hbm, agg), (targ_hbm, targ))
    loads = [
        pltpu.make_async_copy(source, dest, load_sem.at[n])
        for n, (source, dest) in enumerate(operands)
    ]
    for load in loads:
        load.start()

    def iota(rows, columns):
        shape = (rows, columns)
        return (lax.broadcasted_iota(jnp.int32, shape, 0), lax.broadcasted_iota(jnp.int32, shape, 1))

    def ones_where(condition):
        return jnp.where(condition, 1.0, 0.0).astype(BF16)

    low = iota(ROWS, LANES)[1] < B
    low_block = iota(B, LANES)[1] < B
    low_tiles = iota(TILES, LANES)[1] < B
    low_row = low[:8]

    row, column = iota(HALF, HALF)
    turn = ones_where((row >> 4 == (column & 15)) & ((row & 15) == column >> 4))
    row, column = iota(2 * HALF, HALF)
    turn_twice = ones_where((row >> 5 == (column & 15)) & ((row >> 1 & 15) == column >> 4))

    def stack(tile):
        return jnp.concatenate([tile(t) for t in range(ROWS)], axis=0)

    loads[0].wait()
    flat = jnp.concatenate(
        [
            stack(lambda t, half=half: p_raw[:, pl.ds((half * ROWS + t) * LANES, LANES)])
            for half in range(2)
        ],
        axis=1,
    )
    doubled = jnp.dot(turn_twice, flat, preferred_element_type=F32)
    first_row = (iota(TILES, LANES)[0] & 1) == 0
    for j in range(ROWS // 2):
        for half in range(2):
            lanes = slice(half * LANES, (half + 1) * LANES)
            one = doubled[j * TILES : (j + 1) * TILES, lanes]
            two = doubled[(j + 8) * TILES : (j + 9) * TILES, lanes]
            left = jnp.where(first_row, one, swap(one))
            right = jnp.where(first_row, swap(two), two)
            own_pairs[j, pl.ds(half * TILES, TILES), :] = jnp.where(low_tiles, left, right).astype(BF16)

    def remote(source, dest, n, device):
        return pltpu.make_async_remote_copy(
            source, dest, send_sem.at[n], recv_sem.at[n], device_id=device, device_id_type=MESH
        )

    to_far = remote(own_pairs, far_pairs, 0, send_to)
    to_sib = remote(own_pairs, sib_pairs, 1, sibling)
    to_relay = remote(own_pairs, passing, 3, send_to)
    to_pass = pltpu.make_async_remote_copy(
        passing, far_pairs, send_sem.at[4], recv_sem.at[0], device_id=pass_to, device_id_type=MESH
    )

    def send_far():
        pl.when(jnp.logical_not(relayed))(to_far.start)
        pl.when(relayed)(to_relay.start)

    @pl.when(at_once)
    def _():
        pl.semaphore_wait(barrier, expected)
        send_far()
        to_sib.start()

    loads[1].wait()
    for n, (k, other) in enumerate(PAIRS):
        for half in range(2):

            def tile(t, which, half=half):
                return a_raw[which, :, pl.ds((half * ROWS + t) * LANES, LANES)]

            def side(h, t, k=k, other=other, tile=tile):
                one = tile(t, k)[:, h * B : (h + 1) * B]
                two = jnp.zeros_like(one) if other is None else tile(t, other)[:, h * B : (h + 1) * B]
                return jnp.concatenate([one, two], axis=1)

            both = jnp.concatenate(
                [stack(functools.partial(side, h)) for h in range(2)], axis=1
            )
            turned = jnp.dot(turn, both, preferred_element_type=F32).astype(BF16)
            for h in range(2):
                blocks[n, 2 * h + half] = turned[:, h * LANES : (h + 1) * LANES]

    def unpack(source, left, right, start):
        def one(j, carry):
            both = source[j].astype(F32)
            turned = swap(both)
            left[start + j] = jnp.where(low_block, both, 0.0).astype(BF16)
            right[start + j] = jnp.where(low_block, 0.0, turned).astype(BF16)
            left[start + j + 8] = jnp.where(low_block, turned, 0.0).astype(BF16)
            right[start + j + 8] = jnp.where(low_block, 0.0, both).astype(BF16)
            return carry

        lax.fori_loop(0, ROWS // 2, one, 0, unroll=2)

    def clear(left, right, start):
        def one(j, carry):
            left[start + j] = jnp.zeros((B, LANES), BF16)
            right[start + j] = jnp.zeros((B, LANES), BF16)
            return carry

        lax.fori_loop(0, ROWS, one, 0, unroll=4)

    far_start = 2 * ROWS * core
    sib_start = 2 * ROWS - far_start
    clear(near_left, near_right, far_start)
    clear(far_left, far_right, ROWS)
    clear(far_left, far_right, sib_start)
    unpack(own_pairs, near_left, near_right, ROWS)

    for load in loads[2:]:
        load.wait()
    first = me - core
    together = jnp.dot(turn, flat, preferred_element_type=F32)
    p_f32[0] = together[:, :LANES]
    p_f32[1] = together[:, LANES:]

    def mask(i, carry):
        keep = [jnp.where(agg[i] == first + c, 1.0, 0.0) for c in range(2)]
        for half in range(2):
            x = p_f32[half, pl.ds(pl.multiple_of(i * ROWS, ROWS), ROWS), :]
            y = swap(x)
            masked[i, pl.ds(half * ROWS, ROWS), :] = jnp.where(low, x * keep[0], y * keep[1]).astype(BF16)
            masked[i, pl.ds(TILES + half * ROWS, ROWS), :] = jnp.where(
                low, y * keep[0], x * keep[1]
            ).astype(BF16)
        return carry

    lax.fori_loop(0, ROWS, mask, 0, unroll=4)
    row, column = iota(LANES, LANES)
    order = ones_where(column == (row >> 6 << 6) + 2 * (row & 31) + (row >> 5 & 1))
    masked_t[...] = lax.dot_general(
        order,
        masked[...].reshape(ROWS * B, LANES),
        (((1,), (1,)), ((), ())),
        preferred_element_type=F32,
    ).astype(BF16)

    root = (me - 1) * ROWS

    def entry(k, i):
        return jnp.clip(cols[k, i] - root, 0, 3 * ROWS - 1)

    def multiply(pairs, left, right, half_way):
        def group(g, carry):
            for r in range(GROUP):
                i = g * GROUP + r
                applied, slots = [], []
                for n, (k, other) in pairs:
                    above = left[entry(k, i)]
                    slot = jnp.full((8, LANES), targ[k, i], jnp.int32)
                    if other is None:
                        below = jnp.zeros((B, LANES), BF16)
                    else:
                        below = right[entry(other, i)]
                        slot = jnp.where(low_row, slot, targ[other, i])
                    rows = pl.ds(pl.multiple_of(i * ROWS, ROWS), ROWS)
                    applied.append(
                        jnp.dot(
                            jnp.concatenate([blocks[n, q, rows, :] for q in range(4)], axis=0),
                            jnp.concatenate([above, below], axis=0),
                            preferred_element_type=F32,
                        )
                    )
                    slots.append(slot)
                for s in range(KC):
                    summed = None
                    for value, slot in zip(applied, slots):
                        keep = jnp.concatenate([jnp.where(slot == s, 1.0, 0.0)] * 8, axis=0)
                        term = value * keep
                        summed = term if summed is None else summed + term
                    y_all[i, :, pl.ds(s * LANES, LANES)] = summed.astype(BF16)
            return carry

        lax.fori_loop(0, 2, group, 0)
        half_way()
        lax.fori_loop(2, ROWS // GROUP, group, 0)
        return jnp.dot(
            masked_t[...],
            y_all[...].reshape(ROWS * B, KC * LANES),
            preferred_element_type=F32,
        )

    numbered = list(enumerate(PAIRS))

    @pl.when(jnp.logical_not(at_once))
    def _():
        pl.semaphore_wait(barrier, expected)
        pl.when(first_wave)(send_far)
        to_sib.start()

    to_sib.wait_recv()
    unpack(sib_pairs, near_left, near_right, sib_start)
    acc[...] = multiply(numbered, near_left, near_right, lambda: pl.when(second_wave)(send_far))

    def far_sent():
        pl.when(jnp.logical_not(relayed))(to_far.wait_send)
        pl.when(relayed)(to_relay.wait_send)

    @pl.when(lets)
    def _():
        far_sent()
        pl.semaphore_signal(go_sem, inc=1, device_id=let_go, device_id_type=MESH)

    @pl.when(passes)
    def _():
        to_relay.wait_recv()
        to_pass.start()

    @pl.when(third_wave)
    def _():
        pl.semaphore_wait(go_sem, 1)
        send_far()

    to_far.wait_recv()
    unpack(far_pairs, far_left, far_right, far_start)
    acc[...] += multiply(numbered[:3], far_left, far_right, lambda: None)

    def folded(c, s):
        even = acc[pl.ds(c * B, TILES), pl.ds(s * LANES, LANES)]
        odd = acc[pl.ds(c * B + TILES, TILES), pl.ds(s * LANES, LANES)]
        return jnp.where(low_tiles, even + swap(even), odd + swap(odd))

    for s in range(KC):
        part_out[s] = folded(1 - core, s)
    to_part = remote(part_out, part_in, 2, sibling)
    to_part.start()
    mine = [folded(core, s) for s in range(KC)]
    to_part.wait_recv()
    for s in range(KC):
        out[s] = mine[s] + part_in[s]
    pl.when(jnp.logical_not(lets))(far_sent)
    pl.when(passes)(to_pass.wait_send)
    for copy in (to_sib, to_part):
        copy.wait_send()


def local(n_wide, n_narrow, a_blocks, p_blocks, columns, aggregate, target):
    hbm = pl.BlockSpec(memory_space=pltpu.HBM)
    vmem = pltpu.VMEM
    smem = pltpu.SMEM
    operands = (columns.T, aggregate, target.T, p_blocks, jnp.transpose(a_blocks, (1, 0, 2)))
    result = pl.pallas_call(
        functools.partial(kernel, n_wide, n_narrow),
        out_shape=jax.ShapeDtypeStruct((KC, TILES, LANES), F32),
        in_specs=[hbm] * 5,
        out_specs=pl.BlockSpec(memory_space=pltpu.VMEM),
        scratch_shapes=[
            smem((K, ROWS), jnp.int32),
            smem((ROWS,), jnp.int32),
            smem((K, ROWS), jnp.int32),
            vmem((ROWS, B * B), BF16),
            vmem((K, ROWS, B * B), BF16),
            vmem((2, HALF, LANES), F32),
            vmem((ROWS // 2, B, LANES), BF16),
            vmem((ROWS // 2, B, LANES), BF16),
            vmem((ROWS // 2, B, LANES), BF16),
            vmem((ROWS // 2, B, LANES), BF16),
            vmem((3 * ROWS, B, LANES), BF16),
            vmem((3 * ROWS, B, LANES), BF16),
            vmem((3 * ROWS, B, LANES), BF16),
            vmem((3 * ROWS, B, LANES), BF16),
            vmem((len(PAIRS), 4, HALF, LANES), BF16),
            vmem((ROWS, B, KC * LANES), BF16),
            vmem((ROWS, B, LANES), BF16),
            vmem((LANES, ROWS * B), BF16),
            vmem((LANES, KC * LANES), F32),
            vmem((KC, TILES, LANES), F32),
            vmem((KC, TILES, LANES), F32),
            pltpu.SemaphoreType.DMA((5,)),
            pltpu.SemaphoreType.DMA((5,)),
            pltpu.SemaphoreType.DMA((5,)),
            pltpu.SemaphoreType.REGULAR,
        ],
        compiler_params=pltpu.CompilerParams(
            collective_id=0, has_side_effects=True, vmem_limit_bytes=40 * 2**20
        ),
    )(*(pltpu.with_memory_space_constraint(value, pltpu.HBM) for value in operands))
    return result.reshape(1, KC, B * B)


def solution(mesh):
    placed = (
        P(("wide", "narrow"), None, None),
        P(("wide", "narrow"), None),
        P(("wide", "narrow"), None),
        P(("wide", "narrow")),
        P(("wide", "narrow"), None),
    )
    return jax.shard_map(
        functools.partial(local, mesh.shape["wide"], mesh.shape["narrow"]),
        mesh=mesh,
        in_specs=placed,
        out_specs=P(("wide", "narrow"), None, None),
        check_vma=False,
    )
```

```python
import functools

import jax
import jax.numpy as jnp
from jax import lax
from jax.experimental import pallas as pl
from jax.experimental.pallas import tpu as pltpu
from jax.sharding import PartitionSpec as P

B = 64
K = 7
KC = 7
ROWS = 16
TILES = 32
LANES = 128
HALF = 256
PAIRS = ((1, 2), (3, 4), (5, 6), (0, None))
GROUP = 4
X_CHIPS = 4
F32 = jnp.float32
BF16 = jnp.bfloat16
MESH = pl.DeviceIdType.MESH


def swap(x):
    return pltpu.roll(x, B, 1)


def kernel(
    n_wide,
    n_narrow,
    cols_hbm,
    agg_hbm,
    targ_hbm,
    p_hbm,
    a_hbm,
    out,
    cols,
    agg,
    targ,
    p_raw,
    a_raw,
    p_f32,
    own_pairs,
    sib_pairs,
    far_pairs,
    passing,
    near_left,
    near_right,
    far_left,
    far_right,
    blocks,
    y_all,
    masked,
    masked_t,
    acc,
    part_out,
    part_in,
    load_sem,
    send_sem,
    recv_sem,
):
    total = n_wide * n_narrow
    me = lax.axis_index("wide") * n_narrow + lax.axis_index("narrow")
    core = me % 2

    def place(index):
        return (index // n_narrow, index % n_narrow)

    def far_of(index):
        return (index - 1 + 2 * (index % 2) + total) % total

    wide, narrow = me // n_narrow, me % n_narrow
    x, z_lo = wide % X_CHIPS, wide // X_CHIPS
    z_run = n_wide // X_CHIPS
    last_x, last = X_CHIPS - 1, n_narrow - 1

    def both(*conditions):
        return functools.reduce(jnp.logical_and, conditions)

    def pick(condition, one, two):
        return tuple(jnp.where(condition, a, b) for a, b in zip(one, two))

    quarter = z_run // 4
    first_wave = jnp.logical_or(z_lo < 2 * quarter, me == total - 1)
    at_once = jnp.logical_and(first_wave, narrow // 2 % 2 == 1)
    second_wave = jnp.logical_and(z_lo >= 2 * quarter, z_lo < 3 * quarter)
    third_wave = jnp.logical_and(z_lo >= 3 * quarter, me != total - 1)

    odd = z_lo % 2 == 1
    above = both(narrow == last, x == last_x, z_lo < z_run - 1, odd)
    below = both(narrow == 0, x == 0, z_lo > 0, jnp.logical_not(odd))
    relayed = jnp.logical_or(above, below)
    by_above = both(narrow == last - 1, x == last_x, z_lo > 2, odd)
    by_below = both(narrow == 1, x == 0, z_lo < z_run - 3, jnp.logical_not(odd))
    passes = jnp.logical_or(by_above, by_below)
    far = place(far_of(me))
    on_above = ((z_lo + 2) * X_CHIPS + last_x, last - 1)
    on_below = ((z_lo - 2) * X_CHIPS, 1)
    send_to = pick(above, on_above, pick(below, on_below, far))
    come_from = pick(above, ((z_lo - 1) * X_CHIPS, 1), pick(below, ((z_lo + 1) * X_CHIPS + last_x, last - 1), far))
    pass_from = pick(by_above, ((z_lo - 2) * X_CHIPS + last_x, last), ((z_lo + 2) * X_CHIPS, 0))
    pass_to = pick(by_above, ((z_lo - 1) * X_CHIPS, 0), ((z_lo + 1) * X_CHIPS + last_x, last))
    sibling = place(me + 1 - 2 * core)

    barrier = pltpu.get_barrier_semaphore()

    def greet(other):
        pl.semaphore_signal(barrier, inc=1, device_id=other, device_id_type=MESH)

    greet(sibling)
    greet(come_from)
    pl.when(passes)(functools.partial(greet, pass_from))
    expected = 2 + jnp.where(passes, 1, 0)
    operands = ((p_hbm, p_raw), (a_hbm, a_raw), (cols_hbm, cols), (agg_hbm, agg), (targ_hbm, targ))
    loads = [
        pltpu.make_async_copy(source, dest, load_sem.at[n])
        for n, (source, dest) in enumerate(operands)
    ]
    for load in loads:
        load.start()

    def iota(rows, columns):
        shape = (rows, columns)
        return (lax.broadcasted_iota(jnp.int32, shape, 0), lax.broadcasted_iota(jnp.int32, shape, 1))

    def ones_where(condition):
        return jnp.where(condition, 1.0, 0.0).astype(BF16)

    low = iota(ROWS, LANES)[1] < B
    low_block = iota(B, LANES)[1] < B
    low_tiles = iota(TILES, LANES)[1] < B
    low_row = low[:8]

    row, column = iota(HALF, HALF)
    turn = ones_where((row >> 4 == (column & 15)) & ((row & 15) == column >> 4))
    row, column = iota(2 * HALF, HALF)
    turn_twice = ones_where((row >> 5 == (column & 15)) & ((row >> 1 & 15) == column >> 4))

    def stack(tile):
        return jnp.concatenate([tile(t) for t in range(ROWS)], axis=0)

    loads[0].wait()
    flat = jnp.concatenate(
        [
            stack(lambda t, half=half: p_raw[:, pl.ds((half * ROWS + t) * LANES, LANES)])
            for half in range(2)
        ],
        axis=1,
    )
    doubled = jnp.dot(turn_twice, flat, preferred_element_type=F32)
    first_row = (iota(TILES, LANES)[0] & 1) == 0
    for j in range(ROWS // 2):
        for half in range(2):
            lanes = slice(half * LANES, (half + 1) * LANES)
            one = doubled[j * TILES : (j + 1) * TILES, lanes]
            two = doubled[(j + 8) * TILES : (j + 9) * TILES, lanes]
            left = jnp.where(first_row, one, swap(one))
            right = jnp.where(first_row, swap(two), two)
            own_pairs[j, pl.ds(half * TILES, TILES), :] = jnp.where(low_tiles, left, right).astype(BF16)

    def remote(source, dest, n, device):
        return pltpu.make_async_remote_copy(
            source, dest, send_sem.at[n], recv_sem.at[n], device_id=device, device_id_type=MESH
        )

    to_far = remote(own_pairs, far_pairs, 0, send_to)
    to_sib = remote(own_pairs, sib_pairs, 1, sibling)
    to_relay = remote(own_pairs, passing, 3, send_to)
    to_pass = pltpu.make_async_remote_copy(
        passing, far_pairs, send_sem.at[4], recv_sem.at[0], device_id=pass_to, device_id_type=MESH
    )

    def send_far():
        pl.when(jnp.logical_not(relayed))(to_far.start)
        pl.when(relayed)(to_relay.start)

    @pl.when(at_once)
    def _():
        pl.semaphore_wait(barrier, expected)
        send_far()
        to_sib.start()

    loads[1].wait()
    for n, (k, other) in enumerate(PAIRS):
        for half in range(2):

            def tile(t, which, half=half):
                return a_raw[which, :, pl.ds((half * ROWS + t) * LANES, LANES)]

            def side(h, t, k=k, other=other, tile=tile):
                one = tile(t, k)[:, h * B : (h + 1) * B]
                two = jnp.zeros_like(one) if other is None else tile(t, other)[:, h * B : (h + 1) * B]
                return jnp.concatenate([one, two], axis=1)

            both = jnp.concatenate(
                [stack(functools.partial(side, h)) for h in range(2)], axis=1
            )
            turned = jnp.dot(turn, both, preferred_element_type=F32).astype(BF16)
            for h in range(2):
                blocks[n, 2 * h + half] = turned[:, h * LANES : (h + 1) * LANES]

    def unpack(source, left, right, start):
        def one(j, carry):
            both = source[j].astype(F32)
            turned = swap(both)
            left[start + j] = jnp.where(low_block, both, 0.0).astype(BF16)
            right[start + j] = jnp.where(low_block, 0.0, turned).astype(BF16)
            left[start + j + 8] = jnp.where(low_block, turned, 0.0).astype(BF16)
            right[start + j + 8] = jnp.where(low_block, 0.0, both).astype(BF16)
            return carry

        lax.fori_loop(0, ROWS // 2, one, 0, unroll=2)

    def clear(left, right, start):
        def one(j, carry):
            left[start + j] = jnp.zeros((B, LANES), BF16)
            right[start + j] = jnp.zeros((B, LANES), BF16)
            return carry

        lax.fori_loop(0, ROWS, one, 0, unroll=4)

    far_start = 2 * ROWS * core
    sib_start = 2 * ROWS - far_start
    clear(near_left, near_right, far_start)
    clear(far_left, far_right, ROWS)
    clear(far_left, far_right, sib_start)
    unpack(own_pairs, near_left, near_right, ROWS)

    for load in loads[2:]:
        load.wait()
    first = me - core
    together = jnp.dot(turn, flat, preferred_element_type=F32)
    p_f32[0] = together[:, :LANES]
    p_f32[1] = together[:, LANES:]

    def mask(i, carry):
        keep = [jnp.where(agg[i] == first + c, 1.0, 0.0) for c in range(2)]
        for half in range(2):
            x = p_f32[half, pl.ds(pl.multiple_of(i * ROWS, ROWS), ROWS), :]
            y = swap(x)
            masked[i, pl.ds(half * ROWS, ROWS), :] = jnp.where(low, x * keep[0], y * keep[1]).astype(BF16)
            masked[i, pl.ds(TILES + half * ROWS, ROWS), :] = jnp.where(
                low, y * keep[0], x * keep[1]
            ).astype(BF16)
        return carry

    lax.fori_loop(0, ROWS, mask, 0, unroll=4)
    row, column = iota(LANES, LANES)
    order = ones_where(column == (row >> 6 << 6) + 2 * (row & 31) + (row >> 5 & 1))
    masked_t[...] = lax.dot_general(
        order,
        masked[...].reshape(ROWS * B, LANES),
        (((1,), (1,)), ((), ())),
        preferred_element_type=F32,
    ).astype(BF16)

    root = (me - 1) * ROWS

    def entry(k, i):
        return jnp.clip(cols[k, i] - root, 0, 3 * ROWS - 1)

    def multiply(pairs, left, right, half_way):
        def group(g, carry):
            for r in range(GROUP):
                i = g * GROUP + r
                applied, slots = [], []
                for n, (k, other) in pairs:
                    above = left[entry(k, i)]
                    slot = jnp.full((8, LANES), targ[k, i], jnp.int32)
                    if other is None:
                        below = jnp.zeros((B, LANES), BF16)
                    else:
                        below = right[entry(other, i)]
                        slot = jnp.where(low_row, slot, targ[other, i])
                    rows = pl.ds(pl.multiple_of(i * ROWS, ROWS), ROWS)
                    applied.append(
                        jnp.dot(
                            jnp.concatenate([blocks[n, q, rows, :] for q in range(4)], axis=0),
                            jnp.concatenate([above, below], axis=0),
                            preferred_element_type=F32,
                        )
                    )
                    slots.append(slot)
                for s in range(KC):
                    summed = None
                    for value, slot in zip(applied, slots):
                        keep = jnp.concatenate([jnp.where(slot == s, 1.0, 0.0)] * 8, axis=0)
                        term = value * keep
                        summed = term if summed is None else summed + term
                    y_all[i, :, pl.ds(s * LANES, LANES)] = summed.astype(BF16)
            return carry

        lax.fori_loop(0, 2, group, 0)
        half_way()
        lax.fori_loop(2, ROWS // GROUP, group, 0)
        return jnp.dot(
            masked_t[...],
            y_all[...].reshape(ROWS * B, KC * LANES),
            preferred_element_type=F32,
        )

    numbered = list(enumerate(PAIRS))

    @pl.when(jnp.logical_not(at_once))
    def _():
        pl.semaphore_wait(barrier, expected)
        pl.when(first_wave)(send_far)
        to_sib.start()

    to_sib.wait_recv()
    unpack(sib_pairs, near_left, near_right, sib_start)
    acc[...] = multiply(numbered, near_left, near_right, lambda: pl.when(second_wave)(send_far))

    pl.when(third_wave)(send_far)

    @pl.when(passes)
    def _():
        to_relay.wait_recv()
        to_pass.start()

    to_far.wait_recv()
    unpack(far_pairs, far_left, far_right, far_start)
    acc[...] += multiply(numbered[:3], far_left, far_right, lambda: None)

    def folded(c, s):
        even = acc[pl.ds(c * B, TILES), pl.ds(s * LANES, LANES)]
        odd = acc[pl.ds(c * B + TILES, TILES), pl.ds(s * LANES, LANES)]
        return jnp.where(low_tiles, even + swap(even), odd + swap(odd))

    for s in range(KC):
        part_out[s] = folded(1 - core, s)
    to_part = remote(part_out, part_in, 2, sibling)
    to_part.start()
    mine = [folded(core, s) for s in range(KC)]
    to_part.wait_recv()
    for s in range(KC):
        out[s] = mine[s] + part_in[s]
    pl.when(jnp.logical_not(relayed))(to_far.wait_send)
    pl.when(relayed)(to_relay.wait_send)
    pl.when(passes)(to_pass.wait_send)
    for copy in (to_sib, to_part):
        copy.wait_send()


def local(n_wide, n_narrow, a_blocks, p_blocks, columns, aggregate, target):
    hbm = pl.BlockSpec(memory_space=pltpu.HBM)
    vmem = pltpu.VMEM
    smem = pltpu.SMEM
    operands = (columns.T, aggregate, target.T, p_blocks, jnp.transpose(a_blocks, (1, 0, 2)))
    result = pl.pallas_call(
        functools.partial(kernel, n_wide, n_narrow),
        out_shape=jax.ShapeDtypeStruct((KC, TILES, LANES), F32),
        in_specs=[hbm] * 5,
        out_specs=pl.BlockSpec(memory_space=pltpu.VMEM),
        scratch_shapes=[
            smem((K, ROWS), jnp.int32),
            smem((ROWS,), jnp.int32),
            smem((K, ROWS), jnp.int32),
            vmem((ROWS, B * B), BF16),
            vmem((K, ROWS, B * B), BF16),
            vmem((2, HALF, LANES), F32),
            vmem((ROWS // 2, B, LANES), BF16),
            vmem((ROWS // 2, B, LANES), BF16),
            vmem((ROWS // 2, B, LANES), BF16),
            vmem((ROWS // 2, B, LANES), BF16),
            vmem((3 * ROWS, B, LANES), BF16),
            vmem((3 * ROWS, B, LANES), BF16),
            vmem((3 * ROWS, B, LANES), BF16),
            vmem((3 * ROWS, B, LANES), BF16),
            vmem((len(PAIRS), 4, HALF, LANES), BF16),
            vmem((ROWS, B, KC * LANES), BF16),
            vmem((ROWS, B, LANES), BF16),
            vmem((LANES, ROWS * B), BF16),
            vmem((LANES, KC * LANES), F32),
            vmem((KC, TILES, LANES), F32),
            vmem((KC, TILES, LANES), F32),
            pltpu.SemaphoreType.DMA((5,)),
            pltpu.SemaphoreType.DMA((5,)),
            pltpu.SemaphoreType.DMA((5,)),
        ],
        compiler_params=pltpu.CompilerParams(
            collective_id=0, has_side_effects=True, vmem_limit_bytes=40 * 2**20
        ),
    )(*(pltpu.with_memory_space_constraint(value, pltpu.HBM) for value in operands))
    return result.reshape(1, KC, B * B)


def solution(mesh):
    placed = (
        P(("wide", "narrow"), None, None),
        P(("wide", "narrow"), None),
        P(("wide", "narrow"), None),
        P(("wide", "narrow")),
        P(("wide", "narrow"), None),
    )
    return jax.shard_map(
        functools.partial(local, mesh.shape["wide"], mesh.shape["narrow"]),
        mesh=mesh,
        in_specs=placed,
        out_specs=P(("wide", "narrow"), None, None),
        check_vma=False,
    )
```

```python
import functools

import jax
import jax.numpy as jnp
from jax import lax
from jax.experimental import pallas as pl
from jax.experimental.pallas import tpu as pltpu
from jax.sharding import PartitionSpec as P

B = 64
K = 7
KC = 7
ROWS = 16
TILES = 32
LANES = 128
HALF = 256
PAIRS = ((1, 2), (3, 4), (5, 6), (0, None))
GROUP = 4
X_CHIPS = 4
F32 = jnp.float32
BF16 = jnp.bfloat16
MESH = pl.DeviceIdType.MESH


def swap(x):
    return pltpu.roll(x, B, 1)


def kernel(
    n_wide,
    n_narrow,
    cols_hbm,
    agg_hbm,
    targ_hbm,
    p_hbm,
    a_hbm,
    out,
    cols,
    agg,
    targ,
    p_raw,
    a_raw,
    p_f32,
    own_pairs,
    sib_pairs,
    far_pairs,
    passing,
    near_left,
    near_right,
    far_left,
    far_right,
    blocks,
    y_all,
    masked,
    masked_t,
    acc,
    part_out,
    part_in,
    load_sem,
    send_sem,
    recv_sem,
):
    total = n_wide * n_narrow
    me = lax.axis_index("wide") * n_narrow + lax.axis_index("narrow")
    core = me % 2

    def place(index):
        return (index // n_narrow, index % n_narrow)

    def far_of(index):
        return (index - 1 + 2 * (index % 2) + total) % total

    wide, narrow = me // n_narrow, me % n_narrow
    x, z_lo = wide % X_CHIPS, wide // X_CHIPS
    z_run = n_wide // X_CHIPS
    last_x, last = X_CHIPS - 1, n_narrow - 1

    def both(*conditions):
        return functools.reduce(jnp.logical_and, conditions)

    def pick(condition, one, two):
        return tuple(jnp.where(condition, a, b) for a, b in zip(one, two))

    quarter = z_run // 4
    odd = z_lo % 2 == 1
    above = both(narrow == last, x == last_x, z_lo < z_run - 1, odd)
    below = both(narrow == 0, x == 0, z_lo > 0, jnp.logical_not(odd))
    relayed = jnp.logical_or(above, below)
    by_above = both(narrow == last - 1, x == last_x, z_lo > 2, odd)
    by_below = both(narrow == 1, x == 0, z_lo < z_run - 3, jnp.logical_not(odd))
    first_wave = jnp.logical_or(relayed, jnp.logical_or(z_lo < 2 * quarter, me == total - 1))
    at_once = jnp.logical_and(first_wave, narrow // 2 % 2 == 1)
    second_wave = jnp.logical_and(jnp.logical_not(first_wave), z_lo < 3 * quarter)
    third_wave = jnp.logical_and(jnp.logical_not(first_wave), z_lo >= 3 * quarter)
    passes = jnp.logical_or(by_above, by_below)
    far = place(far_of(me))
    on_above = ((z_lo + 2) * X_CHIPS + last_x, last - 1)
    on_below = ((z_lo - 2) * X_CHIPS, 1)
    send_to = pick(above, on_above, pick(below, on_below, far))
    come_from = pick(above, ((z_lo - 1) * X_CHIPS, 1), pick(below, ((z_lo + 1) * X_CHIPS + last_x, last - 1), far))
    pass_from = pick(by_above, ((z_lo - 2) * X_CHIPS + last_x, last), ((z_lo + 2) * X_CHIPS, 0))
    pass_to = pick(by_above, ((z_lo - 1) * X_CHIPS, 0), ((z_lo + 1) * X_CHIPS + last_x, last))
    sibling = place(me + 1 - 2 * core)

    barrier = pltpu.get_barrier_semaphore()

    def greet(other):
        pl.semaphore_signal(barrier, inc=1, device_id=other, device_id_type=MESH)

    greet(sibling)
    greet(come_from)
    pl.when(passes)(functools.partial(greet, pass_from))
    expected = 2 + jnp.where(passes, 1, 0)
    operands = ((p_hbm, p_raw), (a_hbm, a_raw), (cols_hbm, cols), (agg_hbm, agg), (targ_hbm, targ))
    loads = [
        pltpu.make_async_copy(source, dest, load_sem.at[n])
        for n, (source, dest) in enumerate(operands)
    ]
    for load in loads:
        load.start()

    def iota(rows, columns):
        shape = (rows, columns)
        return (lax.broadcasted_iota(jnp.int32, shape, 0), lax.broadcasted_iota(jnp.int32, shape, 1))

    def ones_where(condition):
        return jnp.where(condition, 1.0, 0.0).astype(BF16)

    low = iota(ROWS, LANES)[1] < B
    low_block = iota(B, LANES)[1] < B
    low_tiles = iota(TILES, LANES)[1] < B
    low_row = low[:8]

    row, column = iota(HALF, HALF)
    turn = ones_where((row >> 4 == (column & 15)) & ((row & 15) == column >> 4))
    row, column = iota(2 * HALF, HALF)
    turn_twice = ones_where((row >> 5 == (column & 15)) & ((row >> 1 & 15) == column >> 4))

    def stack(tile):
        return jnp.concatenate([tile(t) for t in range(ROWS)], axis=0)

    loads[0].wait()
    flat = jnp.concatenate(
        [
            stack(lambda t, half=half: p_raw[:, pl.ds((half * ROWS + t) * LANES, LANES)])
            for half in range(2)
        ],
        axis=1,
    )
    doubled = jnp.dot(turn_twice, flat, preferred_element_type=F32)
    first_row = (iota(TILES, LANES)[0] & 1) == 0
    for j in range(ROWS // 2):
        for half in range(2):
            lanes = slice(half * LANES, (half + 1) * LANES)
            one = doubled[j * TILES : (j + 1) * TILES, lanes]
            two = doubled[(j + 8) * TILES : (j + 9) * TILES, lanes]
            left = jnp.where(first_row, one, swap(one))
            right = jnp.where(first_row, swap(two), two)
            own_pairs[j, pl.ds(half * TILES, TILES), :] = jnp.where(low_tiles, left, right).astype(BF16)

    def remote(source, dest, n, device):
        return pltpu.make_async_remote_copy(
            source, dest, send_sem.at[n], recv_sem.at[n], device_id=device, device_id_type=MESH
        )

    to_far = remote(own_pairs, far_pairs, 0, send_to)
    to_sib = remote(own_pairs, sib_pairs, 1, sibling)
    to_relay = remote(own_pairs, passing, 3, send_to)
    to_pass = pltpu.make_async_remote_copy(
        passing, far_pairs, send_sem.at[4], recv_sem.at[0], device_id=pass_to, device_id_type=MESH
    )

    def send_far():
        pl.when(jnp.logical_not(relayed))(to_far.start)
        pl.when(relayed)(to_relay.start)

    @pl.when(at_once)
    def _():
        pl.semaphore_wait(barrier, expected)
        send_far()
        to_sib.start()

    loads[1].wait()
    for n, (k, other) in enumerate(PAIRS):
        for half in range(2):

            def tile(t, which, half=half):
                return a_raw[which, :, pl.ds((half * ROWS + t) * LANES, LANES)]

            def side(h, t, k=k, other=other, tile=tile):
                one = tile(t, k)[:, h * B : (h + 1) * B]
                two = jnp.zeros_like(one) if other is None else tile(t, other)[:, h * B : (h + 1) * B]
                return jnp.concatenate([one, two], axis=1)

            both = jnp.concatenate(
                [stack(functools.partial(side, h)) for h in range(2)], axis=1
            )
            turned = jnp.dot(turn, both, preferred_element_type=F32).astype(BF16)
            for h in range(2):
                blocks[n, 2 * h + half] = turned[:, h * LANES : (h + 1) * LANES]

    def unpack(source, left, right, start):
        def one(j, carry):
            both = source[j].astype(F32)
            turned = swap(both)
            left[start + j] = jnp.where(low_block, both, 0.0).astype(BF16)
            right[start + j] = jnp.where(low_block, 0.0, turned).astype(BF16)
            left[start + j + 8] = jnp.where(low_block, turned, 0.0).astype(BF16)
            right[start + j + 8] = jnp.where(low_block, 0.0, both).astype(BF16)
            return carry

        lax.fori_loop(0, ROWS // 2, one, 0, unroll=2)

    def clear(left, right, start):
        def one(j, carry):
            left[start + j] = jnp.zeros((B, LANES), BF16)
            right[start + j] = jnp.zeros((B, LANES), BF16)
            return carry

        lax.fori_loop(0, ROWS, one, 0, unroll=4)

    far_start = 2 * ROWS * core
    sib_start = 2 * ROWS - far_start
    clear(near_left, near_right, far_start)
    clear(far_left, far_right, ROWS)
    clear(far_left, far_right, sib_start)
    unpack(own_pairs, near_left, near_right, ROWS)

    for load in loads[2:]:
        load.wait()
    first = me - core
    together = jnp.dot(turn, flat, preferred_element_type=F32)
    p_f32[0] = together[:, :LANES]
    p_f32[1] = together[:, LANES:]

    def mask(i, carry):
        keep = [jnp.where(agg[i] == first + c, 1.0, 0.0) for c in range(2)]
        for half in range(2):
            x = p_f32[half, pl.ds(pl.multiple_of(i * ROWS, ROWS), ROWS), :]
            y = swap(x)
            masked[i, pl.ds(half * ROWS, ROWS), :] = jnp.where(low, x * keep[0], y * keep[1]).astype(BF16)
            masked[i, pl.ds(TILES + half * ROWS, ROWS), :] = jnp.where(
                low, y * keep[0], x * keep[1]
            ).astype(BF16)
        return carry

    lax.fori_loop(0, ROWS, mask, 0, unroll=4)
    row, column = iota(LANES, LANES)
    order = ones_where(column == (row >> 6 << 6) + 2 * (row & 31) + (row >> 5 & 1))
    masked_t[...] = lax.dot_general(
        order,
        masked[...].reshape(ROWS * B, LANES),
        (((1,), (1,)), ((), ())),
        preferred_element_type=F32,
    ).astype(BF16)

    root = (me - 1) * ROWS

    def entry(k, i):
        return jnp.clip(cols[k, i] - root, 0, 3 * ROWS - 1)

    def multiply(pairs, left, right, half_way):
        def group(g, carry):
            for r in range(GROUP):
                i = g * GROUP + r
                applied, slots = [], []
                for n, (k, other) in pairs:
                    above = left[entry(k, i)]
                    slot = jnp.full((8, LANES), targ[k, i], jnp.int32)
                    if other is None:
                        below = jnp.zeros((B, LANES), BF16)
                    else:
                        below = right[entry(other, i)]
                        slot = jnp.where(low_row, slot, targ[other, i])
                    rows = pl.ds(pl.multiple_of(i * ROWS, ROWS), ROWS)
                    applied.append(
                        jnp.dot(
                            jnp.concatenate([blocks[n, q, rows, :] for q in range(4)], axis=0),
                            jnp.concatenate([above, below], axis=0),
                            preferred_element_type=F32,
                        )
                    )
                    slots.append(slot)
                for s in range(KC):
                    summed = None
                    for value, slot in zip(applied, slots):
                        keep = jnp.concatenate([jnp.where(slot == s, 1.0, 0.0)] * 8, axis=0)
                        term = value * keep
                        summed = term if summed is None else summed + term
                    y_all[i, :, pl.ds(s * LANES, LANES)] = summed.astype(BF16)
            return carry

        lax.fori_loop(0, 2, group, 0)
        half_way()
        lax.fori_loop(2, ROWS // GROUP, group, 0)
        return jnp.dot(
            masked_t[...],
            y_all[...].reshape(ROWS * B, KC * LANES),
            preferred_element_type=F32,
        )

    numbered = list(enumerate(PAIRS))

    @pl.when(jnp.logical_not(at_once))
    def _():
        pl.semaphore_wait(barrier, expected)
        pl.when(first_wave)(send_far)
        to_sib.start()

    to_sib.wait_recv()
    unpack(sib_pairs, near_left, near_right, sib_start)
    def half_way():
        pl.when(second_wave)(send_far)

        @pl.when(passes)
        def _():
            to_relay.wait_recv()
            to_pass.start()

    acc[...] = multiply(numbered, near_left, near_right, half_way)

    pl.when(third_wave)(send_far)

    to_far.wait_recv()
    unpack(far_pairs, far_left, far_right, far_start)
    acc[...] += multiply(numbered[:3], far_left, far_right, lambda: None)

    def folded(c, s):
        even = acc[pl.ds(c * B, TILES), pl.ds(s * LANES, LANES)]
        odd = acc[pl.ds(c * B + TILES, TILES), pl.ds(s * LANES, LANES)]
        return jnp.where(low_tiles, even + swap(even), odd + swap(odd))

    for s in range(KC):
        part_out[s] = folded(1 - core, s)
    to_part = remote(part_out, part_in, 2, sibling)
    to_part.start()
    mine = [folded(core, s) for s in range(KC)]
    to_part.wait_recv()
    for s in range(KC):
        out[s] = mine[s] + part_in[s]
    pl.when(jnp.logical_not(relayed))(to_far.wait_send)
    pl.when(relayed)(to_relay.wait_send)
    pl.when(passes)(to_pass.wait_send)
    for copy in (to_sib, to_part):
        copy.wait_send()


def local(n_wide, n_narrow, a_blocks, p_blocks, columns, aggregate, target):
    hbm = pl.BlockSpec(memory_space=pltpu.HBM)
    vmem = pltpu.VMEM
    smem = pltpu.SMEM
    operands = (columns.T, aggregate, target.T, p_blocks, jnp.transpose(a_blocks, (1, 0, 2)))
    result = pl.pallas_call(
        functools.partial(kernel, n_wide, n_narrow),
        out_shape=jax.ShapeDtypeStruct((KC, TILES, LANES), F32),
        in_specs=[hbm] * 5,
        out_specs=pl.BlockSpec(memory_space=pltpu.VMEM),
        scratch_shapes=[
            smem((K, ROWS), jnp.int32),
            smem((ROWS,), jnp.int32),
            smem((K, ROWS), jnp.int32),
            vmem((ROWS, B * B), BF16),
            vmem((K, ROWS, B * B), BF16),
            vmem((2, HALF, LANES), F32),
            vmem((ROWS // 2, B, LANES), BF16),
            vmem((ROWS // 2, B, LANES), BF16),
            vmem((ROWS // 2, B, LANES), BF16),
            vmem((ROWS // 2, B, LANES), BF16),
            vmem((3 * ROWS, B, LANES), BF16),
            vmem((3 * ROWS, B, LANES), BF16),
            vmem((3 * ROWS, B, LANES), BF16),
            vmem((3 * ROWS, B, LANES), BF16),
            vmem((len(PAIRS), 4, HALF, LANES), BF16),
            vmem((ROWS, B, KC * LANES), BF16),
            vmem((ROWS, B, LANES), BF16),
            vmem((LANES, ROWS * B), BF16),
            vmem((LANES, KC * LANES), F32),
            vmem((KC, TILES, LANES), F32),
            vmem((KC, TILES, LANES), F32),
            pltpu.SemaphoreType.DMA((5,)),
            pltpu.SemaphoreType.DMA((5,)),
            pltpu.SemaphoreType.DMA((5,)),
        ],
        compiler_params=pltpu.CompilerParams(
            collective_id=0, has_side_effects=True, vmem_limit_bytes=40 * 2**20
        ),
    )(*(pltpu.with_memory_space_constraint(value, pltpu.HBM) for value in operands))
    return result.reshape(1, KC, B * B)


def solution(mesh):
    placed = (
        P(("wide", "narrow"), None, None),
        P(("wide", "narrow"), None),
        P(("wide", "narrow"), None),
        P(("wide", "narrow")),
        P(("wide", "narrow"), None),
    )
    return jax.shard_map(
        functools.partial(local, mesh.shape["wide"], mesh.shape["narrow"]),
        mesh=mesh,
        in_specs=placed,
        out_specs=P(("wide", "narrow"), None, None),
        check_vma=False,
    )
```

```python
import functools

import jax
import jax.numpy as jnp
from jax import lax
from jax.experimental import pallas as pl
from jax.experimental.pallas import tpu as pltpu
from jax.sharding import PartitionSpec as P

B = 64
K = 7
KC = 7
ROWS = 16
TILES = 32
LANES = 128
HALF = 256
PAIRS = ((1, 2), (3, 4), (5, 6), (0, None))
GROUP = 4
X_CHIPS = 4
F32 = jnp.float32
BF16 = jnp.bfloat16
MESH = pl.DeviceIdType.MESH


def swap(x):
    return pltpu.roll(x, B, 1)


def kernel(
    n_wide,
    n_narrow,
    cols_hbm,
    agg_hbm,
    targ_hbm,
    p_hbm,
    a_hbm,
    out,
    cols,
    agg,
    targ,
    p_raw,
    a_raw,
    p_f32,
    own_pairs,
    sib_pairs,
    far_pairs,
    passing,
    near_left,
    near_right,
    far_left,
    far_right,
    blocks,
    y_all,
    masked,
    masked_t,
    acc,
    part_out,
    part_in,
    load_sem,
    send_sem,
    recv_sem,
):
    total = n_wide * n_narrow
    me = lax.axis_index("wide") * n_narrow + lax.axis_index("narrow")
    core = me % 2

    def place(index):
        return (index // n_narrow, index % n_narrow)

    def far_of(index):
        return (index - 1 + 2 * (index % 2) + total) % total

    wide, narrow = me // n_narrow, me % n_narrow
    x, z_lo = wide % X_CHIPS, wide // X_CHIPS
    z_run = n_wide // X_CHIPS
    last_x, last = X_CHIPS - 1, n_narrow - 1

    def both(*conditions):
        return functools.reduce(jnp.logical_and, conditions)

    def pick(condition, one, two):
        return tuple(jnp.where(condition, a, b) for a, b in zip(one, two))

    quarter = z_run // 4
    odd = z_lo % 2 == 1
    above = both(narrow == last, x == last_x, z_lo < z_run - 1, odd)
    below = both(narrow == 0, x == 0, z_lo > 0, jnp.logical_not(odd))
    relayed = jnp.logical_or(above, below)
    by_above = both(narrow == last - 1, x == last_x, z_lo > 2, odd)
    by_below = both(narrow == 1, x == 0, z_lo < z_run - 3, jnp.logical_not(odd))
    first_wave = jnp.logical_or(relayed, jnp.logical_or(z_lo < 2 * quarter, me == total - 1))
    at_once = jnp.logical_and(first_wave, narrow // 2 % 2 == 1)
    second_wave = jnp.logical_and(jnp.logical_not(first_wave), z_lo < 3 * quarter)
    third_wave = jnp.logical_and(jnp.logical_not(first_wave), z_lo >= 3 * quarter)
    passes = jnp.logical_or(by_above, by_below)
    far = place(far_of(me))
    on_above = ((z_lo + 2) * X_CHIPS + last_x, last - 1)
    on_below = ((z_lo - 2) * X_CHIPS, 1)
    send_to = pick(above, on_above, pick(below, on_below, far))
    come_from = pick(above, ((z_lo - 1) * X_CHIPS, 1), pick(below, ((z_lo + 1) * X_CHIPS + last_x, last - 1), far))
    pass_from = pick(by_above, ((z_lo - 2) * X_CHIPS + last_x, last), ((z_lo + 2) * X_CHIPS, 0))
    pass_to = pick(by_above, ((z_lo - 1) * X_CHIPS, 0), ((z_lo + 1) * X_CHIPS + last_x, last))
    sibling = place(me + 1 - 2 * core)

    barrier = pltpu.get_barrier_semaphore()

    def greet(other):
        pl.semaphore_signal(barrier, inc=1, device_id=other, device_id_type=MESH)

    greet(sibling)
    greet(come_from)
    pl.when(passes)(functools.partial(greet, pass_from))
    expected = 2 + jnp.where(passes, 1, 0)
    operands = ((p_hbm, p_raw), (a_hbm, a_raw), (cols_hbm, cols), (agg_hbm, agg), (targ_hbm, targ))
    loads = [
        pltpu.make_async_copy(source, dest, load_sem.at[n])
        for n, (source, dest) in enumerate(operands)
    ]
    for load in loads:
        load.start()

    def iota(rows, columns):
        shape = (rows, columns)
        return (lax.broadcasted_iota(jnp.int32, shape, 0), lax.broadcasted_iota(jnp.int32, shape, 1))

    def ones_where(condition):
        return jnp.where(condition, 1.0, 0.0).astype(BF16)

    low = iota(ROWS, LANES)[1] < B
    low_block = iota(B, LANES)[1] < B
    low_tiles = iota(TILES, LANES)[1] < B
    low_row = low[:8]

    row, column = iota(HALF, HALF)
    turn = ones_where((row >> 4 == (column & 15)) & ((row & 15) == column >> 4))
    row, column = iota(2 * HALF, HALF)
    turn_twice = ones_where((row >> 5 == (column & 15)) & ((row >> 1 & 15) == column >> 4))

    def stack(tile):
        return jnp.concatenate([tile(t) for t in range(ROWS)], axis=0)

    loads[0].wait()
    flat = jnp.concatenate(
        [
            stack(lambda t, half=half: p_raw[:, pl.ds((half * ROWS + t) * LANES, LANES)])
            for half in range(2)
        ],
        axis=1,
    )
    doubled = jnp.dot(turn_twice, flat, preferred_element_type=F32)
    first_row = (iota(TILES, LANES)[0] & 1) == 0
    for j in range(ROWS // 2):
        for half in range(2):
            lanes = slice(half * LANES, (half + 1) * LANES)
            one = doubled[j * TILES : (j + 1) * TILES, lanes]
            two = doubled[(j + 8) * TILES : (j + 9) * TILES, lanes]
            left = jnp.where(first_row, one, swap(one))
            right = jnp.where(first_row, swap(two), two)
            own_pairs[j, pl.ds(half * TILES, TILES), :] = jnp.where(low_tiles, left, right).astype(BF16)

    def remote(source, dest, n, device):
        return pltpu.make_async_remote_copy(
            source, dest, send_sem.at[n], recv_sem.at[n], device_id=device, device_id_type=MESH
        )

    to_far = remote(own_pairs, far_pairs, 0, send_to)
    to_sib = remote(own_pairs, sib_pairs, 1, sibling)
    to_relay = remote(own_pairs, passing, 3, send_to)
    to_pass = pltpu.make_async_remote_copy(
        passing, far_pairs, send_sem.at[4], recv_sem.at[0], device_id=pass_to, device_id_type=MESH
    )

    def send_far():
        pl.when(jnp.logical_not(relayed))(to_far.start)
        pl.when(relayed)(to_relay.start)

    @pl.when(at_once)
    def _():
        pl.semaphore_wait(barrier, expected)
        send_far()
        to_sib.start()

    loads[1].wait()
    for n, (k, other) in enumerate(PAIRS):
        for half in range(2):

            def tile(t, which, half=half):
                return a_raw[which, :, pl.ds((half * ROWS + t) * LANES, LANES)]

            def side(h, t, k=k, other=other, tile=tile):
                one = tile(t, k)[:, h * B : (h + 1) * B]
                two = jnp.zeros_like(one) if other is None else tile(t, other)[:, h * B : (h + 1) * B]
                return jnp.concatenate([one, two], axis=1)

            both = jnp.concatenate(
                [stack(functools.partial(side, h)) for h in range(2)], axis=1
            )
            turned = jnp.dot(turn, both, preferred_element_type=F32).astype(BF16)
            for h in range(2):
                blocks[n, 2 * h + half] = turned[:, h * LANES : (h + 1) * LANES]

    def unpack(source, left, right, start):
        def one(j, carry):
            both = source[j].astype(F32)
            turned = swap(both)
            left[start + j] = jnp.where(low_block, both, 0.0).astype(BF16)
            right[start + j] = jnp.where(low_block, 0.0, turned).astype(BF16)
            left[start + j + 8] = jnp.where(low_block, turned, 0.0).astype(BF16)
            right[start + j + 8] = jnp.where(low_block, 0.0, both).astype(BF16)
            return carry

        lax.fori_loop(0, ROWS // 2, one, 0, unroll=2)

    def clear(left, right, start):
        def one(j, carry):
            left[start + j] = jnp.zeros((B, LANES), BF16)
            right[start + j] = jnp.zeros((B, LANES), BF16)
            return carry

        lax.fori_loop(0, ROWS, one, 0, unroll=4)

    far_start = 2 * ROWS * core
    sib_start = 2 * ROWS - far_start
    clear(near_left, near_right, far_start)
    clear(far_left, far_right, ROWS)
    clear(far_left, far_right, sib_start)
    unpack(own_pairs, near_left, near_right, ROWS)

    for load in loads[2:]:
        load.wait()
    first = me - core
    together = jnp.dot(turn, flat, preferred_element_type=F32)
    p_f32[0] = together[:, :LANES]
    p_f32[1] = together[:, LANES:]

    def mask(i, carry):
        keep = [jnp.where(agg[i] == first + c, 1.0, 0.0) for c in range(2)]
        for half in range(2):
            x = p_f32[half, pl.ds(pl.multiple_of(i * ROWS, ROWS), ROWS), :]
            y = swap(x)
            masked[i, pl.ds(half * ROWS, ROWS), :] = jnp.where(low, x * keep[0], y * keep[1]).astype(BF16)
            masked[i, pl.ds(TILES + half * ROWS, ROWS), :] = jnp.where(
                low, y * keep[0], x * keep[1]
            ).astype(BF16)
        return carry

    lax.fori_loop(0, ROWS, mask, 0, unroll=4)
    row, column = iota(LANES, LANES)
    order = ones_where(column == (row >> 6 << 6) + 2 * (row & 31) + (row >> 5 & 1))
    masked_t[...] = lax.dot_general(
        order,
        masked[...].reshape(ROWS * B, LANES),
        (((1,), (1,)), ((), ())),
        preferred_element_type=F32,
    ).astype(BF16)

    root = (me - 1) * ROWS

    def entry(k, i):
        return jnp.clip(cols[k, i] - root, 0, 3 * ROWS - 1)

    def multiply(pairs, left, right, half_way):
        def group(g, carry):
            for r in range(GROUP):
                i = g * GROUP + r
                applied, slots = [], []
                for n, (k, other) in pairs:
                    above = left[entry(k, i)]
                    slot = jnp.full((8, LANES), targ[k, i], jnp.int32)
                    if other is None:
                        below = jnp.zeros((B, LANES), BF16)
                    else:
                        below = right[entry(other, i)]
                        slot = jnp.where(low_row, slot, targ[other, i])
                    rows = pl.ds(pl.multiple_of(i * ROWS, ROWS), ROWS)
                    applied.append(
                        jnp.dot(
                            jnp.concatenate([blocks[n, q, rows, :] for q in range(4)], axis=0),
                            jnp.concatenate([above, below], axis=0),
                            preferred_element_type=F32,
                        )
                    )
                    slots.append(slot)
                for s in range(KC):
                    summed = None
                    for value, slot in zip(applied, slots):
                        keep = jnp.concatenate([jnp.where(slot == s, 1.0, 0.0)] * 8, axis=0)
                        term = value * keep
                        summed = term if summed is None else summed + term
                    y_all[i, :, pl.ds(s * LANES, LANES)] = summed.astype(BF16)
            return carry

        lax.fori_loop(0, 2, group, 0)
        half_way()
        lax.fori_loop(2, ROWS // GROUP, group, 0)
        return jnp.dot(
            masked_t[...],
            y_all[...].reshape(ROWS * B, KC * LANES),
            preferred_element_type=F32,
        )

    numbered = list(enumerate(PAIRS))

    @pl.when(jnp.logical_not(at_once))
    def _():
        pl.semaphore_wait(barrier, expected)
        pl.when(first_wave)(send_far)
        to_sib.start()

    to_sib.wait_recv()
    unpack(sib_pairs, near_left, near_right, sib_start)
    pl.when(second_wave)(send_far)
    def half_way():
        pl.when(third_wave)(send_far)

        @pl.when(passes)
        def _():
            to_relay.wait_recv()
            to_pass.start()

    acc[...] = multiply(numbered, near_left, near_right, half_way)

    to_far.wait_recv()
    unpack(far_pairs, far_left, far_right, far_start)
    acc[...] += multiply(numbered[:3], far_left, far_right, lambda: None)

    def folded(c, s):
        even = acc[pl.ds(c * B, TILES), pl.ds(s * LANES, LANES)]
        odd = acc[pl.ds(c * B + TILES, TILES), pl.ds(s * LANES, LANES)]
        return jnp.where(low_tiles, even + swap(even), odd + swap(odd))

    for s in range(KC):
        part_out[s] = folded(1 - core, s)
    to_part = remote(part_out, part_in, 2, sibling)
    to_part.start()
    mine = [folded(core, s) for s in range(KC)]
    to_part.wait_recv()
    for s in range(KC):
        out[s] = mine[s] + part_in[s]
    pl.when(jnp.logical_not(relayed))(to_far.wait_send)
    pl.when(relayed)(to_relay.wait_send)
    pl.when(passes)(to_pass.wait_send)
    for copy in (to_sib, to_part):
        copy.wait_send()


def local(n_wide, n_narrow, a_blocks, p_blocks, columns, aggregate, target):
    hbm = pl.BlockSpec(memory_space=pltpu.HBM)
    vmem = pltpu.VMEM
    smem = pltpu.SMEM
    operands = (columns.T, aggregate, target.T, p_blocks, jnp.transpose(a_blocks, (1, 0, 2)))
    result = pl.pallas_call(
        functools.partial(kernel, n_wide, n_narrow),
        out_shape=jax.ShapeDtypeStruct((KC, TILES, LANES), F32),
        in_specs=[hbm] * 5,
        out_specs=pl.BlockSpec(memory_space=pltpu.VMEM),
        scratch_shapes=[
            smem((K, ROWS), jnp.int32),
            smem((ROWS,), jnp.int32),
            smem((K, ROWS), jnp.int32),
            vmem((ROWS, B * B), BF16),
            vmem((K, ROWS, B * B), BF16),
            vmem((2, HALF, LANES), F32),
            vmem((ROWS // 2, B, LANES), BF16),
            vmem((ROWS // 2, B, LANES), BF16),
            vmem((ROWS // 2, B, LANES), BF16),
            vmem((ROWS // 2, B, LANES), BF16),
            vmem((3 * ROWS, B, LANES), BF16),
            vmem((3 * ROWS, B, LANES), BF16),
            vmem((3 * ROWS, B, LANES), BF16),
            vmem((3 * ROWS, B, LANES), BF16),
            vmem((len(PAIRS), 4, HALF, LANES), BF16),
            vmem((ROWS, B, KC * LANES), BF16),
            vmem((ROWS, B, LANES), BF16),
            vmem((LANES, ROWS * B), BF16),
            vmem((LANES, KC * LANES), F32),
            vmem((KC, TILES, LANES), F32),
            vmem((KC, TILES, LANES), F32),
            pltpu.SemaphoreType.DMA((5,)),
            pltpu.SemaphoreType.DMA((5,)),
            pltpu.SemaphoreType.DMA((5,)),
        ],
        compiler_params=pltpu.CompilerParams(
            collective_id=0, has_side_effects=True, vmem_limit_bytes=40 * 2**20
        ),
    )(*(pltpu.with_memory_space_constraint(value, pltpu.HBM) for value in operands))
    return result.reshape(1, KC, B * B)


def solution(mesh):
    placed = (
        P(("wide", "narrow"), None, None),
        P(("wide", "narrow"), None),
        P(("wide", "narrow"), None),
        P(("wide", "narrow")),
        P(("wide", "narrow"), None),
    )
    return jax.shard_map(
        functools.partial(local, mesh.shape["wide"], mesh.shape["narrow"]),
        mesh=mesh,
        in_specs=placed,
        out_specs=P(("wide", "narrow"), None, None),
        check_vma=False,
    )
```

```python
import functools

import jax
import jax.numpy as jnp
from jax import lax
from jax.experimental import pallas as pl
from jax.experimental.pallas import tpu as pltpu
from jax.sharding import PartitionSpec as P

B = 64
K = 7
KC = 7
ROWS = 16
TILES = 32
LANES = 128
HALF = 256
PAIRS = ((1, 2), (3, 4), (5, 6), (0, None))
GROUP = 4
X_CHIPS = 4
F32 = jnp.float32
BF16 = jnp.bfloat16
MESH = pl.DeviceIdType.MESH


def swap(x):
    return pltpu.roll(x, B, 1)


def kernel(
    n_wide,
    n_narrow,
    cols_hbm,
    agg_hbm,
    targ_hbm,
    p_hbm,
    a_hbm,
    out,
    cols,
    agg,
    targ,
    p_raw,
    a_raw,
    p_f32,
    own_pairs,
    sib_pairs,
    far_pairs,
    passing,
    near_left,
    near_right,
    far_left,
    far_right,
    blocks,
    y_all,
    masked,
    masked_t,
    acc,
    part_out,
    part_in,
    load_sem,
    send_sem,
    recv_sem,
):
    total = n_wide * n_narrow
    me = lax.axis_index("wide") * n_narrow + lax.axis_index("narrow")
    core = me % 2

    def place(index):
        return (index // n_narrow, index % n_narrow)

    def far_of(index):
        return (index - 1 + 2 * (index % 2) + total) % total

    wide, narrow = me // n_narrow, me % n_narrow
    x, z_lo = wide % X_CHIPS, wide // X_CHIPS
    z_run = n_wide // X_CHIPS
    last_x, last = X_CHIPS - 1, n_narrow - 1

    def both(*conditions):
        return functools.reduce(jnp.logical_and, conditions)

    def pick(condition, one, two):
        return tuple(jnp.where(condition, a, b) for a, b in zip(one, two))

    quarter = z_run // 4
    odd = z_lo % 2 == 1
    above = both(narrow == last, x == last_x, z_lo < z_run - 1, odd)
    below = both(narrow == 0, x == 0, z_lo > 0, jnp.logical_not(odd))
    relayed = jnp.logical_or(above, below)
    by_above = both(narrow == last - 1, x == last_x, z_lo > 2, odd)
    by_below = both(narrow == 1, x == 0, z_lo < z_run - 3, jnp.logical_not(odd))
    first_wave = jnp.logical_or(relayed, jnp.logical_or(z_lo < 2 * quarter - 1, me == total - 1))
    at_once = jnp.logical_and(first_wave, narrow // 2 % 2 == 1)
    second_wave = jnp.logical_and(jnp.logical_not(first_wave), z_lo < 3 * quarter)
    third_wave = jnp.logical_and(jnp.logical_not(first_wave), z_lo >= 3 * quarter)
    passes = jnp.logical_or(by_above, by_below)
    far = place(far_of(me))
    on_above = ((z_lo + 2) * X_CHIPS + last_x, last - 1)
    on_below = ((z_lo - 2) * X_CHIPS, 1)
    send_to = pick(above, on_above, pick(below, on_below, far))
    come_from = pick(above, ((z_lo - 1) * X_CHIPS, 1), pick(below, ((z_lo + 1) * X_CHIPS + last_x, last - 1), far))
    pass_from = pick(by_above, ((z_lo - 2) * X_CHIPS + last_x, last), ((z_lo + 2) * X_CHIPS, 0))
    pass_to = pick(by_above, ((z_lo - 1) * X_CHIPS, 0), ((z_lo + 1) * X_CHIPS + last_x, last))
    sibling = place(me + 1 - 2 * core)

    barrier = pltpu.get_barrier_semaphore()

    def greet(other):
        pl.semaphore_signal(barrier, inc=1, device_id=other, device_id_type=MESH)

    greet(sibling)
    greet(come_from)
    pl.when(passes)(functools.partial(greet, pass_from))
    expected = 2 + jnp.where(passes, 1, 0)
    operands = ((p_hbm, p_raw), (a_hbm, a_raw), (cols_hbm, cols), (agg_hbm, agg), (targ_hbm, targ))
    loads = [
        pltpu.make_async_copy(source, dest, load_sem.at[n])
        for n, (source, dest) in enumerate(operands)
    ]
    for load in loads:
        load.start()

    def iota(rows, columns):
        shape = (rows, columns)
        return (lax.broadcasted_iota(jnp.int32, shape, 0), lax.broadcasted_iota(jnp.int32, shape, 1))

    def ones_where(condition):
        return jnp.where(condition, 1.0, 0.0).astype(BF16)

    low = iota(ROWS, LANES)[1] < B
    low_block = iota(B, LANES)[1] < B
    low_tiles = iota(TILES, LANES)[1] < B
    low_row = low[:8]

    row, column = iota(HALF, HALF)
    turn = ones_where((row >> 4 == (column & 15)) & ((row & 15) == column >> 4))
    row, column = iota(2 * HALF, HALF)
    turn_twice = ones_where((row >> 5 == (column & 15)) & ((row >> 1 & 15) == column >> 4))

    def stack(tile):
        return jnp.concatenate([tile(t) for t in range(ROWS)], axis=0)

    loads[0].wait()
    flat = jnp.concatenate(
        [
            stack(lambda t, half=half: p_raw[:, pl.ds((half * ROWS + t) * LANES, LANES)])
            for half in range(2)
        ],
        axis=1,
    )
    doubled = jnp.dot(turn_twice, flat, preferred_element_type=F32)
    first_row = (iota(TILES, LANES)[0] & 1) == 0
    for j in range(ROWS // 2):
        for half in range(2):
            lanes = slice(half * LANES, (half + 1) * LANES)
            one = doubled[j * TILES : (j + 1) * TILES, lanes]
            two = doubled[(j + 8) * TILES : (j + 9) * TILES, lanes]
            left = jnp.where(first_row, one, swap(one))
            right = jnp.where(first_row, swap(two), two)
            own_pairs[j, pl.ds(half * TILES, TILES), :] = jnp.where(low_tiles, left, right).astype(BF16)

    def remote(source, dest, n, device):
        return pltpu.make_async_remote_copy(
            source, dest, send_sem.at[n], recv_sem.at[n], device_id=device, device_id_type=MESH
        )

    to_far = remote(own_pairs, far_pairs, 0, send_to)
    to_sib = remote(own_pairs, sib_pairs, 1, sibling)
    to_relay = remote(own_pairs, passing, 3, send_to)
    to_pass = pltpu.make_async_remote_copy(
        passing, far_pairs, send_sem.at[4], recv_sem.at[0], device_id=pass_to, device_id_type=MESH
    )

    def send_far():
        pl.when(jnp.logical_not(relayed))(to_far.start)
        pl.when(relayed)(to_relay.start)

    @pl.when(at_once)
    def _():
        pl.semaphore_wait(barrier, expected)
        send_far()
        to_sib.start()

    loads[1].wait()
    for n, (k, other) in enumerate(PAIRS):
        for half in range(2):

            def tile(t, which, half=half):
                return a_raw[which, :, pl.ds((half * ROWS + t) * LANES, LANES)]

            def side(h, t, k=k, other=other, tile=tile):
                one = tile(t, k)[:, h * B : (h + 1) * B]
                two = jnp.zeros_like(one) if other is None else tile(t, other)[:, h * B : (h + 1) * B]
                return jnp.concatenate([one, two], axis=1)

            both = jnp.concatenate(
                [stack(functools.partial(side, h)) for h in range(2)], axis=1
            )
            turned = jnp.dot(turn, both, preferred_element_type=F32).astype(BF16)
            for h in range(2):
                blocks[n, 2 * h + half] = turned[:, h * LANES : (h + 1) * LANES]

    def unpack(source, left, right, start):
        def one(j, carry):
            both = source[j].astype(F32)
            turned = swap(both)
            left[start + j] = jnp.where(low_block, both, 0.0).astype(BF16)
            right[start + j] = jnp.where(low_block, 0.0, turned).astype(BF16)
            left[start + j + 8] = jnp.where(low_block, turned, 0.0).astype(BF16)
            right[start + j + 8] = jnp.where(low_block, 0.0, both).astype(BF16)
            return carry

        lax.fori_loop(0, ROWS // 2, one, 0, unroll=2)

    def clear(left, right, start):
        def one(j, carry):
            left[start + j] = jnp.zeros((B, LANES), BF16)
            right[start + j] = jnp.zeros((B, LANES), BF16)
            return carry

        lax.fori_loop(0, ROWS, one, 0, unroll=4)

    far_start = 2 * ROWS * core
    sib_start = 2 * ROWS - far_start
    clear(near_left, near_right, far_start)
    clear(far_left, far_right, ROWS)
    clear(far_left, far_right, sib_start)
    unpack(own_pairs, near_left, near_right, ROWS)

    for load in loads[2:]:
        load.wait()
    first = me - core
    together = jnp.dot(turn, flat, preferred_element_type=F32)
    p_f32[0] = together[:, :LANES]
    p_f32[1] = together[:, LANES:]

    def mask(i, carry):
        keep = [jnp.where(agg[i] == first + c, 1.0, 0.0) for c in range(2)]
        for half in range(2):
            x = p_f32[half, pl.ds(pl.multiple_of(i * ROWS, ROWS), ROWS), :]
            y = swap(x)
            masked[i, pl.ds(half * ROWS, ROWS), :] = jnp.where(low, x * keep[0], y * keep[1]).astype(BF16)
            masked[i, pl.ds(TILES + half * ROWS, ROWS), :] = jnp.where(
                low, y * keep[0], x * keep[1]
            ).astype(BF16)
        return carry

    lax.fori_loop(0, ROWS, mask, 0, unroll=4)
    row, column = iota(LANES, LANES)
    order = ones_where(column == (row >> 6 << 6) + 2 * (row & 31) + (row >> 5 & 1))
    masked_t[...] = lax.dot_general(
        order,
        masked[...].reshape(ROWS * B, LANES),
        (((1,), (1,)), ((), ())),
        preferred_element_type=F32,
    ).astype(BF16)

    root = (me - 1) * ROWS

    def entry(k, i):
        return jnp.clip(cols[k, i] - root, 0, 3 * ROWS - 1)

    def multiply(pairs, left, right, half_way):
        def group(g, carry):
            for r in range(GROUP):
                i = g * GROUP + r
                applied, slots = [], []
                for n, (k, other) in pairs:
                    above = left[entry(k, i)]
                    slot = jnp.full((8, LANES), targ[k, i], jnp.int32)
                    if other is None:
                        below = jnp.zeros((B, LANES), BF16)
                    else:
                        below = right[entry(other, i)]
                        slot = jnp.where(low_row, slot, targ[other, i])
                    rows = pl.ds(pl.multiple_of(i * ROWS, ROWS), ROWS)
                    applied.append(
                        jnp.dot(
                            jnp.concatenate([blocks[n, q, rows, :] for q in range(4)], axis=0),
                            jnp.concatenate([above, below], axis=0),
                            preferred_element_type=F32,
                        )
                    )
                    slots.append(slot)
                for s in range(KC):
                    summed = None
                    for value, slot in zip(applied, slots):
                        keep = jnp.concatenate([jnp.where(slot == s, 1.0, 0.0)] * 8, axis=0)
                        term = value * keep
                        summed = term if summed is None else summed + term
                    y_all[i, :, pl.ds(s * LANES, LANES)] = summed.astype(BF16)
            return carry

        lax.fori_loop(0, 2, group, 0)
        half_way()
        lax.fori_loop(2, ROWS // GROUP, group, 0)
        return jnp.dot(
            masked_t[...],
            y_all[...].reshape(ROWS * B, KC * LANES),
            preferred_element_type=F32,
        )

    numbered = list(enumerate(PAIRS))

    @pl.when(jnp.logical_not(at_once))
    def _():
        pl.semaphore_wait(barrier, expected)
        pl.when(first_wave)(send_far)
        to_sib.start()

    to_sib.wait_recv()
    unpack(sib_pairs, near_left, near_right, sib_start)
    pl.when(second_wave)(send_far)
    def half_way():
        pl.when(third_wave)(send_far)

        @pl.when(passes)
        def _():
            to_relay.wait_recv()
            to_pass.start()

    acc[...] = multiply(numbered, near_left, near_right, half_way)

    to_far.wait_recv()
    unpack(far_pairs, far_left, far_right, far_start)
    acc[...] += multiply(numbered[:3], far_left, far_right, lambda: None)

    def folded(c, s):
        even = acc[pl.ds(c * B, TILES), pl.ds(s * LANES, LANES)]
        odd = acc[pl.ds(c * B + TILES, TILES), pl.ds(s * LANES, LANES)]
        return jnp.where(low_tiles, even + swap(even), odd + swap(odd))

    for s in range(KC):
        part_out[s] = folded(1 - core, s)
    to_part = remote(part_out, part_in, 2, sibling)
    to_part.start()
    mine = [folded(core, s) for s in range(KC)]
    to_part.wait_recv()
    for s in range(KC):
        out[s] = mine[s] + part_in[s]
    pl.when(jnp.logical_not(relayed))(to_far.wait_send)
    pl.when(relayed)(to_relay.wait_send)
    pl.when(passes)(to_pass.wait_send)
    for copy in (to_sib, to_part):
        copy.wait_send()


def local(n_wide, n_narrow, a_blocks, p_blocks, columns, aggregate, target):
    hbm = pl.BlockSpec(memory_space=pltpu.HBM)
    vmem = pltpu.VMEM
    smem = pltpu.SMEM
    operands = (columns.T, aggregate, target.T, p_blocks, jnp.transpose(a_blocks, (1, 0, 2)))
    result = pl.pallas_call(
        functools.partial(kernel, n_wide, n_narrow),
        out_shape=jax.ShapeDtypeStruct((KC, TILES, LANES), F32),
        in_specs=[hbm] * 5,
        out_specs=pl.BlockSpec(memory_space=pltpu.VMEM),
        scratch_shapes=[
            smem((K, ROWS), jnp.int32),
            smem((ROWS,), jnp.int32),
            smem((K, ROWS), jnp.int32),
            vmem((ROWS, B * B), BF16),
            vmem((K, ROWS, B * B), BF16),
            vmem((2, HALF, LANES), F32),
            vmem((ROWS // 2, B, LANES), BF16),
            vmem((ROWS // 2, B, LANES), BF16),
            vmem((ROWS // 2, B, LANES), BF16),
            vmem((ROWS // 2, B, LANES), BF16),
            vmem((3 * ROWS, B, LANES), BF16),
            vmem((3 * ROWS, B, LANES), BF16),
            vmem((3 * ROWS, B, LANES), BF16),
            vmem((3 * ROWS, B, LANES), BF16),
            vmem((len(PAIRS), 4, HALF, LANES), BF16),
            vmem((ROWS, B, KC * LANES), BF16),
            vmem((ROWS, B, LANES), BF16),
            vmem((LANES, ROWS * B), BF16),
            vmem((LANES, KC * LANES), F32),
            vmem((KC, TILES, LANES), F32),
            vmem((KC, TILES, LANES), F32),
            pltpu.SemaphoreType.DMA((5,)),
            pltpu.SemaphoreType.DMA((5,)),
            pltpu.SemaphoreType.DMA((5,)),
        ],
        compiler_params=pltpu.CompilerParams(
            collective_id=0, has_side_effects=True, vmem_limit_bytes=40 * 2**20
        ),
    )(*(pltpu.with_memory_space_constraint(value, pltpu.HBM) for value in operands))
    return result.reshape(1, KC, B * B)


def solution(mesh):
    placed = (
        P(("wide", "narrow"), None, None),
        P(("wide", "narrow"), None),
        P(("wide", "narrow"), None),
        P(("wide", "narrow")),
        P(("wide", "narrow"), None),
    )
    return jax.shard_map(
        functools.partial(local, mesh.shape["wide"], mesh.shape["narrow"]),
        mesh=mesh,
        in_specs=placed,
        out_specs=P(("wide", "narrow"), None, None),
        check_vma=False,
    )
```
